512 devices in a mesh: dp: 8 (over x, z_hi), ctx: 64 (over y, z_lo, core).
Axes of the slice: x: 4, y: 4, z: 16 (z_hi: 2, z_lo: 8; z = z_hi * 8 + z_lo), core: 2. Of those that a mesh axis runs over, the one named last changes fastest.
Arguments:
- inputs: float32 [8, 2048, 8192], P('dp', None, 'ctx'), may hold values from -6 to 6
- grad_out: float32 [8, 2048, 8192], P('dp', None, 'ctx'), may hold values from -6 to 6
- filters: float32 [2048, 8192], P(('dp', 'ctx')), may hold values from -0.0625 to 0.0625
Outputs:
- input_grad: float32 [8, 2048, 8192], P('dp', None, 'ctx')
- filter_grad: float32 [2048, 8192], P(('dp', 'ctx'))
The draws below stay inside these ranges and needn't reach their ends.
All inputs are finite; a program needn't handle non-finite values.
Results may differ from the reference program's by a relative error of at most 0.000098.
Values sent between devices are 32-bit elements; how exact they have to be, the bound alone decides.
No kernel may reach another device: no remote copies, remote signals or barrier semaphores. Data moves between devices by JAX's collectives and lax.ppermute only.
A program may use at most 64 MiB of HBM per device.

```python
import math
import jax
import jax.numpy as jnp
from jax import lax

D = 2048
L = 8192
SEQS = 8


def shard_levels(stream_key, shape, shards, low, top_value):
    factor_of, own = 1.0, jax.random.fold_in(stream_key, 6)
    for axis_at, parts in shards:
        steps = jnp.exp(jax.random.uniform(jax.random.fold_in(own, axis_at), (parts,), jnp.float32, low / len(shards), top_value / len(shards)))
        factor_of = factor_of * jnp.repeat(steps, shape[axis_at] // parts).reshape([-1 if axis == axis_at else 1 for axis in range(len(shape))])
    return factor_of


def centred(own_key, shape, spread, bound, split=(), dtype=jnp.bfloat16):
    result = spread * jax.random.normal(own_key, shape, jnp.float32)
    if split:
        result = result * shard_levels(own_key, shape, split, -0.22, 0.18)
    return jnp.clip(result, -bound, bound).astype(dtype)


def setup_inputs(seed: int = 0) -> dict:
    streams_of = jax.random.split(jax.random.key(seed), 4)
    inputs = centred(streams_of[0], (SEQS, D, L), 1.0, 6.0, ((0, 8), (2, 64)), jnp.float32)
    grad_out = centred(streams_of[1], (SEQS, D, L), 1.0, 6.0, ((0, 8), (2, 64)), jnp.float32)
    filters = centred(streams_of[2], (D, L), L ** -0.5, 0.0625, ((0, 512),), jnp.float32)
    return dict(inputs=inputs, grad_out=grad_out, filters=filters)


def reference(inputs, grad_out, filters):
    padded_size = 2 * L
    block_width = 128
    blocks = D // block_width
    input_blocks = jnp.moveaxis(inputs.reshape(SEQS, blocks, block_width, L), 1, 0)
    grad_blocks = jnp.moveaxis(grad_out.reshape(SEQS, blocks, block_width, L), 1, 0)
    filter_blocks = filters.reshape(blocks, block_width, L)
    norm_factor = 1.0 / math.sqrt(SEQS * L)

    def one_block(items):
        input_part, grad_part, filter_part = items
        input_spec = jnp.fft.rfft(input_part, n=padded_size, axis=-1)
        grad_spec = jnp.fft.rfft(grad_part, n=padded_size, axis=-1)
        filter_spec = jnp.fft.rfft(filter_part, n=padded_size, axis=-1)
        input_term = jnp.fft.irfft(grad_spec * jnp.conj(filter_spec)[None], n=padded_size, axis=-1)[..., :L]
        corr_spec = lax.optimization_barrier(jnp.sum(grad_spec * jnp.conj(input_spec), axis=0))
        filter_term = jnp.fft.irfft(corr_spec, n=padded_size, axis=-1)[..., :L]
        return (input_term.astype(jnp.float32), (filter_term * norm_factor).astype(jnp.float32))
    input_terms, filter_terms = lax.map(one_block, (input_blocks, grad_blocks, filter_blocks))
    input_grad = jnp.moveaxis(input_terms, 0, 1).reshape(SEQS, D, L)
    filter_grad = filter_terms.reshape(D, L)
    return (input_grad, filter_grad)
```

```python
import math

import jax
import jax.numpy as jnp
import numpy as np
from jax import lax
from jax.experimental import pallas as pl
from jax.experimental.pallas import tpu as pltpu
from jax.sharding import Mesh
from jax.sharding import PartitionSpec as P

INNER = 128
HIGH = lax.Precision.HIGH


def dft_tables(seq_length):
    padded = 2 * seq_length
    outer = padded // INNER
    rows = seq_length // INNER
    freqs = outer // 2 + 1
    row, freq, inner = np.arange(rows), np.arange(freqs), np.arange(INNER)
    angle = 2.0 * np.pi / outer * (row[:, None] * freq[None, :] % outer)
    cos_outer, sin_outer = np.cos(angle), np.sin(angle)
    first = np.concatenate([cos_outer, -sin_outer], axis=1)
    weights = np.where((freq == 0) | (freq == freqs - 1), 1.0, 2.0) / padded
    last = np.concatenate([cos_outer * weights, -sin_outer * weights], axis=1)
    angle = 2.0 * np.pi / INNER * (inner[:, None] * inner[None, :] % INNER)
    cos_inner, sin_inner = np.cos(angle), np.sin(angle)
    forward = np.block([[cos_inner, -sin_inner], [sin_inner, cos_inner]])
    inverse = np.block([[cos_inner, sin_inner], [-sin_inner, cos_inner]])
    angle = 2.0 * np.pi / padded * (freq[:, None] * inner[None, :] % padded)
    return [
        np.asarray(t, np.float32)
        for t in (first, last, forward, inverse, np.cos(angle), np.sin(angle))
    ]


def forward_spectrum(signal, first_table, tables, form):
    _, _, forward, _, cos_turn, sin_turn = tables
    freqs = cos_turn.shape[0]
    first = jnp.einsum(form, signal, first_table, precision=HIGH)
    real, imag = first[:, :, :freqs], first[:, :, freqs:]
    turned = jnp.concatenate(
        [real * cos_turn + imag * sin_turn, imag * cos_turn - real * sin_turn], axis=-1
    )
    return jnp.einsum("bhkn,nj->bhkj", turned, forward, precision=HIGH)


def inverse_signal(real, imag, last_table, tables, form):
    _, _, _, inverse, cos_turn, sin_turn = tables
    stacked = jnp.concatenate([real, imag], axis=-1)
    middle = jnp.einsum("bhkj,jn->bhkn", stacked, inverse, precision=HIGH)
    middle_real, middle_imag = middle[..., :INNER], middle[..., INNER:]
    back = jnp.concatenate(
        [
            middle_real * cos_turn - middle_imag * sin_turn,
            middle_imag * cos_turn + middle_real * sin_turn,
        ],
        axis=2,
    )
    return jnp.einsum(form, back, last_table, precision=HIGH)


def pack_kernel(half, grad, tokens, blocks):
    _, _, y, z, _, _ = tokens.shape
    own, far = half[0], 1 - half[0]
    for i in range(y):
        for k in range(z):
            for n, array in enumerate((grad, tokens)):
                blocks[i, k, 0, n] = array[:, own, i, k]
                blocks[i, k, 1, n] = array[:, far, i, z - 1 - k]


def unpack_kernel(half, blocks, tokens):
    _, _, y, z, _, _ = tokens.shape
    own, far = half[0], 1 - half[0]
    for i in range(y):
        for k in range(z):
            tokens[:, own, i, k] = blocks[i, k, 0]
            tokens[:, far, i, z - 1 - k] = blocks[i, k, 1]


def moving(kernel, half, arrays, shape):
    whole = pl.BlockSpec(memory_space=pltpu.VMEM)
    size = 8 * math.prod(shape)
    return pl.pallas_call(
        kernel,
        out_shape=jax.ShapeDtypeStruct(shape, jnp.float32),
        in_specs=[pl.BlockSpec(memory_space=pltpu.SMEM)] + [whole] * len(arrays),
        out_specs=whole,
        cost_estimate=pl.CostEstimate(flops=0, bytes_accessed=size, transcendentals=0),
    )(half, *arrays)


def shards(inputs, grad_out, filters):
    x, h, y, z, c = (lax.axis_size(a) for a in ("x", "zh", "y", "zl", "c"))
    at_x, half, at_c = (lax.axis_index(a) for a in ("x", "zh", "c"))
    _, channels, block = inputs.shape
    j = channels // (x * h * y * z * c)
    seq_length = filters.shape[1]
    rows = y * z * c
    tables = dft_tables(seq_length)
    norm = 1.0 / math.sqrt(x * h * seq_length)
    first, last = jnp.asarray(tables[0]), jnp.asarray(tables[1]).T
    place = half.reshape(1).astype(jnp.int32)
    whole_shape = (x, h, y, z, c * j, INNER)
    block_shape = (rows, x, c * j, INNER)

    def exchange(blocks):
        return lax.all_to_all(blocks, ("y", "zl", "c"), 0, 0, tiled=True)

    swap = [(0, 1), (1, 0)]
    facing = []
    for i in range(h * z):
        facing += [(c * i, c * i), (c * i + 1, c * (h * z - 1 - i) + 1)]
    along_x = lambda v, s: lax.ppermute(v, "x", [(i, (i + s) % x) for i in range(x)])

    both = moving(
        pack_kernel,
        place,
        [grad_out.reshape(whole_shape), inputs.reshape(whole_shape)],
        (y, z, c, 2, x, c * j, INNER),
    )
    both = exchange(both.reshape(rows, 2, x, c * j, INNER))

    sibling = lax.ppermute(filters, "c", swap)
    tile = jnp.where(
        at_c == 0,
        jnp.concatenate([filters, sibling]),
        jnp.concatenate([sibling, filters]),
    )
    tile = lax.ppermute(tile, ("zh", "zl", "c"), facing)
    tiles = jnp.stack([tile] + [along_x(tile, x - s) for s in range(1, x)])
    tiles = jnp.roll(tiles, at_x, axis=0)
    filter_spec = forward_spectrum(
        tiles.reshape(x, c * j, rows, INNER), first, tables, "xham,ak->xhkm"
    )
    filter_real, filter_imag = filter_spec[..., :INNER], filter_spec[..., INNER:]

    grad_spec = forward_spectrum(both[:, 0], first, tables, "axhm,ak->xhkm")
    grad_real, grad_imag = grad_spec[..., :INNER], grad_spec[..., INNER:]
    input_part = inverse_signal(
        grad_real * filter_real + grad_imag * filter_imag,
        grad_imag * filter_real - grad_real * filter_imag,
        last,
        tables,
        "xhkm,ka->axhm",
    )
    returned = exchange(input_part)

    input_spec = forward_spectrum(both[:, 1], first, tables, "axhm,ak->xhkm")
    input_real, input_imag = input_spec[..., :INNER], input_spec[..., INNER:]
    filter_part = inverse_signal(
        grad_real * input_real + grad_imag * input_imag,
        grad_imag * input_real - grad_real * input_imag,
        last,
        tables,
        "xhkm,ka->xham",
    )
    parts = jnp.roll(filter_part.reshape(x, c, j, seq_length) * norm, -at_x, axis=0)
    part = parts[0] + sum(along_x(parts[s], s) for s in range(1, x))
    part = lax.ppermute(part, ("zh", "zl", "c"), facing)
    kept = lax.dynamic_index_in_dim(part, at_c, 0, keepdims=False)
    sent = lax.dynamic_index_in_dim(part, 1 - at_c, 0, keepdims=False)
    filter_grad = kept + lax.ppermute(sent, "c", swap)

    blocks = returned.reshape(y, z, c, x, c * j, INNER)
    input_grad = moving(unpack_kernel, place, [blocks], whole_shape)
    return (input_grad.reshape(1, channels, block), filter_grad)


def solution(mesh):
    count = mesh.devices.size
    devices = mesh.devices.reshape(4, 2, 4, count // 64, 2)
    fine = Mesh(devices, ("x", "zh", "y", "zl", "c"))
    tokens = P(("x", "zh"), None, ("y", "zl", "c"))
    owners = P(("x", "zh", "y", "zl", "c"), None)
    return jax.shard_map(
        shards,
        mesh=fine,
        in_specs=(tokens, tokens, owners),
        out_specs=(tokens, owners),
        check_vma=False,
    )
```

```python
import math

import jax
import jax.numpy as jnp
import numpy as np
from jax import lax
from jax.experimental import pallas as pl
from jax.experimental.pallas import tpu as pltpu
from jax.sharding import Mesh
from jax.sharding import PartitionSpec as P

INNER = 128
HALF = 72


def two_parts(table):
    high = np.asarray(table, np.float32).astype(jnp.bfloat16)
    return high, (table - high.astype(np.float64)).astype(jnp.bfloat16)


def dft_tables(seq_length, norm):
    padded = 2 * seq_length
    outer = padded // INNER
    rows = seq_length // INNER
    freqs = outer // 2 + 1
    row, freq, inner = np.arange(rows), np.arange(freqs), np.arange(INNER)
    pad = ((0, HALF - freqs), (0, 0))
    angle = 2.0 * np.pi / outer * (freq[:, None] * row[None, :] % outer)
    cos_outer, sin_outer = np.pad(np.cos(angle), pad), np.pad(np.sin(angle), pad)
    weights = np.where((freq == 0) | (freq == freqs - 1), 1.0, 2.0)[:, None] / padded
    weights = np.pad(weights, pad)
    high, low = two_parts(np.concatenate([cos_outer, -sin_outer], axis=0))
    first = np.concatenate([high, high, low], axis=1)
    last = np.concatenate([cos_outer * weights, -sin_outer * weights], axis=0).T
    angle = 2.0 * np.pi / INNER * (inner[:, None] * inner[None, :] % INNER)
    cos_inner, sin_inner = np.cos(angle), np.sin(angle)
    forward = np.block([[cos_inner, -sin_inner], [sin_inner, cos_inner]])
    inverse = np.block([[cos_inner, sin_inner], [-sin_inner, cos_inner]])
    angle = 2.0 * np.pi / padded * (freq[:, None] * inner[None, :] % padded)
    turn = np.stack([np.pad(np.cos(angle), pad), np.pad(np.sin(angle), pad)])
    pairs = dict(last=last, last_scaled=last * norm, forward=forward, inverse=inverse)
    tables = {name: jnp.asarray(np.stack(two_parts(t))) for name, t in pairs.items()}
    tables["first"] = jnp.asarray(first)
    tables["turn"] = jnp.asarray(turn, jnp.float32)
    return tables


def split(values):
    high = values.astype(jnp.bfloat16)
    return high, (values - high.astype(jnp.float32)).astype(jnp.bfloat16)


def dot(a, b):
    return jnp.dot(a, b, preferred_element_type=jnp.float32)


def forward_spectrum(wide, first, turn, forward):
    high, low = split(wide)
    outer = dot(first[...], jnp.concatenate([high, low, high], axis=0))
    cos, sin = turn[0], turn[1]
    turned = []
    for at in range(0, wide.shape[1], INNER):
        real, imag = outer[:HALF, at : at + INNER], outer[HALF:, at : at + INNER]
        turned.append(
            jnp.concatenate([real * cos + imag * sin, imag * cos - real * sin], axis=1)
        )
    high, low = split(jnp.concatenate(turned, axis=0))
    return dot(high, forward[0]) + (dot(low, forward[0]) + dot(high, forward[1]))


def correlate(spec, other):
    real, imag = spec[:, :INNER], spec[:, INNER:]
    other_real, other_imag = other[:, :INNER], other[:, INNER:]
    return jnp.concatenate(
        [real * other_real + imag * other_imag, imag * other_real - real * other_imag], axis=1
    )


def inverse_signal(spec, inverse, turn, last):
    high, low = split(spec)
    middle = dot(high, inverse[0]) + (dot(low, inverse[0]) + dot(high, inverse[1]))
    cos, sin = turn[0], turn[1]
    back = []
    for at in range(0, spec.shape[0], HALF):
        real, imag = middle[at : at + HALF, :INNER], middle[at : at + HALF, INNER:]
        back.append(
            jnp.concatenate([real * cos - imag * sin, imag * cos + real * sin], axis=0)
        )
    high, low = split(jnp.concatenate(back, axis=1))
    return dot(last[0], high) + (dot(last[0], low) + dot(last[1], high))


def rows_to_wide(block):
    return jnp.concatenate([block[:, r, :] for r in range(block.shape[1])], axis=1)


def filter_kernel(first, turn, forward, filters, spec):
    wide = jnp.concatenate([filters[r] for r in range(filters.shape[0])], axis=1)
    spec[...] = forward_spectrum(wide, first, turn, forward)


def input_grad_kernel(at, first, turn, forward, inverse, last, grad, filter_spec, spec, out):
    spec[...] = forward_spectrum(rows_to_wide(grad), first, turn, forward)
    wide = inverse_signal(correlate(spec[...], filter_spec[...]), inverse, turn, last)
    for r in range(out.shape[1]):
        out[:, r, :] = wide[:, r * INNER : (r + 1) * INNER]


def filter_grad_kernel(at, first, turn, forward, inverse, last, tokens, grad_spec, out):
    spec = forward_spectrum(rows_to_wide(tokens), first, turn, forward)
    wide = inverse_signal(correlate(grad_spec[...], spec), inverse, turn, last)
    for r in range(out.shape[0]):
        out[r] = wide[:, r * INNER : (r + 1) * INNER]


def table_specs(tables, names):
    whole = lambda t: pl.BlockSpec(t.shape, lambda i, *_: (0,) * t.ndim)
    return [whole(tables[n]) for n in names], [tables[n] for n in names]


def cost(flops, size):
    return pl.CostEstimate(flops=flops, bytes_accessed=size, transcendentals=0)


LIMIT = pltpu.CompilerParams(vmem_limit_bytes=48 * 2**20)


def filter_spectrum(filters, tables):
    count, r, a, m = filters.shape
    specs, operands = table_specs(tables, ("first", "turn", "forward"))
    return pl.pallas_call(
        filter_kernel,
        grid=(count,),
        out_shape=jax.ShapeDtypeStruct((count, r * HALF, 2 * m), jnp.float32),
        in_specs=specs + [pl.BlockSpec((None, r, a, m), lambda i: (i, 0, 0, 0))],
        out_specs=pl.BlockSpec((None, r * HALF, 2 * m), lambda i: (i, 0, 0)),
        cost_estimate=cost(10**9, 8 * filters.size),
        compiler_params=LIMIT,
    )(*operands, filters)


def input_grad_part(at_x, both, filter_spec, tables):
    a, _, count, r, m = both.shape
    names = ("first", "turn", "forward", "inverse", "last")
    specs, operands = table_specs(tables, names)
    spec_shape = (None, r * HALF, 2 * m)
    grid_spec = pltpu.PrefetchScalarGridSpec(
        num_scalar_prefetch=1,
        grid=(count,),
        in_specs=specs
        + [
            pl.BlockSpec((a, None, None, r, m), lambda i, at: (0, 0, i, 0, 0)),
            pl.BlockSpec(spec_shape, lambda i, at: ((at[0] - i) & (count - 1), 0, 0)),
        ],
        out_specs=[
            pl.BlockSpec(spec_shape, lambda i, at: (i, 0, 0)),
            pl.BlockSpec((a, None, r, m), lambda i, at: (0, i, 0, 0)),
        ],
    )
    return pl.pallas_call(
        input_grad_kernel,
        grid_spec=grid_spec,
        out_shape=[
            jax.ShapeDtypeStruct((count, r * HALF, 2 * m), jnp.float32),
            jax.ShapeDtypeStruct((a, count, r, m), jnp.float32),
        ],
        cost_estimate=cost(2 * 10**9, 8 * both.size),
        compiler_params=LIMIT,
    )(at_x, *operands, both, filter_spec)


def filter_grad_part(at_x, both, grad_spec, tables):
    a, _, count, r, m = both.shape
    names = ("first", "turn", "forward", "inverse", "last_scaled")
    specs, operands = table_specs(tables, names)
    grid_spec = pltpu.PrefetchScalarGridSpec(
        num_scalar_prefetch=1,
        grid=(count,),
        in_specs=specs
        + [
            pl.BlockSpec((a, None, None, r, m), lambda i, at: (0, 1, i, 0, 0)),
            pl.BlockSpec((None, r * HALF, 2 * m), lambda i, at: (i, 0, 0)),
        ],
        out_specs=pl.BlockSpec(
            (None, r, a, m), lambda i, at: ((i - at[0]) & (count - 1), 0, 0, 0)
        ),
    )
    return pl.pallas_call(
        filter_grad_kernel,
        grid_spec=grid_spec,
        out_shape=jax.ShapeDtypeStruct((count, r, a, m), jnp.float32),
        cost_estimate=cost(0, 0),
        compiler_params=LIMIT,
    )(at_x, *operands, both, grad_spec)


def pack_kernel(half, grad, tokens, blocks):
    _, _, y, z, rows, _ = tokens.shape
    own, far, j = half[0], 1 - half[0], rows // 2
    for i in range(y):
        for k in range(z):
            for n, array in enumerate((grad, tokens)):
                near, other = array[:, own, i, k], array[:, far, i, z - 1 - k]
                blocks[i, k, 0, n] = jnp.concatenate([near[:, :j], other[:, :j]], axis=1)
                blocks[i, k, 1, n] = jnp.concatenate([near[:, j:], other[:, j:]], axis=1)


def unpack_kernel(half, blocks, tokens):
    _, _, y, z, rows, _ = tokens.shape
    own, far, j = half[0], 1 - half[0], rows // 2
    for i in range(y):
        for k in range(z):
            low, high = blocks[i, k, 0], blocks[i, k, 1]
            tokens[:, own, i, k] = jnp.concatenate([low[:, :j], high[:, :j]], axis=1)
            tokens[:, far, i, z - 1 - k] = jnp.concatenate([low[:, j:], high[:, j:]], axis=1)


def moving(kernel, half, arrays, shape):
    whole = pl.BlockSpec(memory_space=pltpu.VMEM)
    return pl.pallas_call(
        kernel,
        out_shape=jax.ShapeDtypeStruct(shape, jnp.float32),
        in_specs=[pl.BlockSpec(memory_space=pltpu.SMEM)] + [whole] * len(arrays),
        out_specs=whole,
        cost_estimate=cost(0, 8 * math.prod(shape)),
    )(half, *arrays)


def shards(inputs, grad_out, filters):
    x, h, y, z, c = (lax.axis_size(a) for a in ("x", "zh", "y", "zl", "c"))
    _, channels, block = inputs.shape
    j = channels // (x * h * y * z * c)
    seq_length = filters.shape[1]
    rows = y * z * c
    tables = dft_tables(seq_length, 1.0 / math.sqrt(x * h * seq_length))
    half = lax.axis_index("zh").reshape(1).astype(jnp.int32)
    at_x = lax.axis_index("x").reshape(1).astype(jnp.int32)
    whole_shape = (x, h, y, z, c * j, INNER)

    def exchange(blocks):
        return lax.all_to_all(blocks, ("y", "zl", "c"), 0, 0, tiled=True)

    def facing(v):
        return lax.ppermute(v, ("zh", "zl"), [(i, h * z - 1 - i) for i in range(h * z)])

    def along_x(v, s):
        return lax.ppermute(v, "x", [(i, (i + s) % x) for i in range(x)])

    both = moving(
        pack_kernel,
        half,
        [grad_out.reshape(whole_shape), inputs.reshape(whole_shape)],
        (y, z, c, 2, x, h * j, INNER),
    )
    both, filters = lax.optimization_barrier((both, filters))
    both = exchange(both.reshape(rows, 2, x, h * j, INNER))

    filters = filters.reshape(j, rows, INNER)
    pair = jnp.concatenate([filters, facing(filters)])
    taps = jnp.stack([pair] + [along_x(pair, s) for s in range(1, x)])
    filter_spec = filter_spectrum(taps, tables)

    grad_spec, leaving = input_grad_part(at_x, both, filter_spec, tables)
    returned = exchange(leaving)

    parts = filter_grad_part(at_x, both, grad_spec, tables)
    part = parts[0] + sum(along_x(parts[s], s) for s in range(1, x))
    filter_grad = part[:j] + facing(part[j:])

    blocks = returned.reshape(y, z, c, x, h * j, INNER)
    input_grad = moving(unpack_kernel, half, [blocks], whole_shape)
    return (input_grad.reshape(1, channels, block), filter_grad.reshape(j, seq_length))


def solution(mesh):
    devices = mesh.devices.reshape(4, 2, 4, -1, 2)
    fine = Mesh(devices, ("x", "zh", "y", "zl", "c"))
    tokens = P(("x", "zh"), None, ("y", "zl", "c"))
    owners = P(("x", "zh", "y", "zl", "c"), None)
    return jax.shard_map(
        shards,
        mesh=fine,
        in_specs=(tokens, tokens, owners),
        out_specs=(tokens, owners),
        check_vma=False,
    )
```

```python
import math

import jax
import jax.numpy as jnp
import numpy as np
from jax import lax
from jax.experimental import pallas as pl
from jax.experimental.pallas import tpu as pltpu
from jax.sharding import Mesh
from jax.sharding import PartitionSpec as P

INNER = 128
HALF = 72


def two_parts(table):
    high = np.asarray(table, np.float32).astype(jnp.bfloat16)
    return high, (table - high.astype(np.float64)).astype(jnp.bfloat16)


def dft_tables(seq_length, norm):
    padded = 2 * seq_length
    outer = padded // INNER
    rows = seq_length // INNER
    freqs = outer // 2 + 1
    row, freq, inner = np.arange(rows), np.arange(freqs), np.arange(INNER)
    pad = ((0, HALF - freqs), (0, 0))
    angle = 2.0 * np.pi / outer * (freq[:, None] * row[None, :] % outer)
    cos_outer, sin_outer = np.pad(np.cos(angle), pad), np.pad(np.sin(angle), pad)
    weights = np.where((freq == 0) | (freq == freqs - 1), 1.0, 2.0)[:, None] / padded
    weights = np.pad(weights, pad)
    high, low = two_parts(np.concatenate([cos_outer, -sin_outer], axis=0))
    first = np.concatenate([high, high, low], axis=1)
    last = np.concatenate([cos_outer * weights, -sin_outer * weights], axis=0).T
    angle = 2.0 * np.pi / INNER * (inner[:, None] * inner[None, :] % INNER)
    cos_inner, sin_inner = np.cos(angle), np.sin(angle)
    forward = np.block([[cos_inner, -sin_inner], [sin_inner, cos_inner]])
    inverse = np.block([[cos_inner, sin_inner], [-sin_inner, cos_inner]])
    angle = 2.0 * np.pi / padded * (freq[:, None] * inner[None, :] % padded)
    turn = np.stack([np.pad(np.cos(angle), pad), np.pad(np.sin(angle), pad)])
    pairs = dict(last=last, last_scaled=last * norm, forward=forward, inverse=inverse)
    tables = {name: jnp.asarray(np.stack(two_parts(t))) for name, t in pairs.items()}
    tables["first"] = jnp.asarray(first)
    tables["turn"] = jnp.asarray(turn, jnp.float32)
    return tables


def split(values):
    high = values.astype(jnp.bfloat16)
    return high, (values - high.astype(jnp.float32)).astype(jnp.bfloat16)


def dot(a, b):
    return jnp.dot(a, b, preferred_element_type=jnp.float32)


def forward_spectrum(wide, first, turn, forward):
    high, low = split(wide)
    outer = dot(first[...], jnp.concatenate([high, low, high], axis=0))
    cos, sin = turn[0], turn[1]
    turned = []
    for at in range(0, wide.shape[1], INNER):
        real, imag = outer[:HALF, at : at + INNER], outer[HALF:, at : at + INNER]
        turned.append(
            jnp.concatenate([real * cos + imag * sin, imag * cos - real * sin], axis=1)
        )
    high, low = split(jnp.concatenate(turned, axis=0))
    return dot(high, forward[0]) + (dot(low, forward[0]) + dot(high, forward[1]))


def correlate(spec, other):
    real, imag = spec[:, :INNER], spec[:, INNER:]
    other_real, other_imag = other[:, :INNER], other[:, INNER:]
    return jnp.concatenate(
        [real * other_real + imag * other_imag, imag * other_real - real * other_imag], axis=1
    )


def inverse_signal(spec, inverse, turn, last):
    high, low = split(spec)
    middle = dot(high, inverse[0]) + (dot(low, inverse[0]) + dot(high, inverse[1]))
    cos, sin = turn[0], turn[1]
    back = []
    for at in range(0, spec.shape[0], HALF):
        real, imag = middle[at : at + HALF, :INNER], middle[at : at + HALF, INNER:]
        back.append(
            jnp.concatenate([real * cos - imag * sin, imag * cos + real * sin], axis=0)
        )
    high, low = split(jnp.concatenate(back, axis=1))
    return dot(last[0], high) + (dot(last[0], low) + dot(last[1], high))


def rows_to_wide(block):
    return jnp.concatenate([block[:, r, :] for r in range(block.shape[1])], axis=1)


def filter_kernel(first, turn, forward, filters, spec):
    wide = jnp.concatenate([filters[r] for r in range(filters.shape[0])], axis=1)
    spec[...] = forward_spectrum(wide, first, turn, forward)


def input_grad_kernel(at, first, turn, forward, inverse, last, grad, filter_spec, spec, out):
    spec[...] = forward_spectrum(rows_to_wide(grad), first, turn, forward)
    wide = inverse_signal(correlate(spec[...], filter_spec[...]), inverse, turn, last)
    for r in range(out.shape[1]):
        out[:, r, :] = wide[:, r * INNER : (r + 1) * INNER]


def filter_grad_kernel(at, first, turn, forward, inverse, last, tokens, grad_spec, out):
    spec = forward_spectrum(rows_to_wide(tokens), first, turn, forward)
    wide = inverse_signal(correlate(grad_spec[...], spec), inverse, turn, last)
    for r in range(out.shape[0]):
        out[r] = wide[:, r * INNER : (r + 1) * INNER]


def table_specs(tables, names):
    whole = lambda t: pl.BlockSpec(t.shape, lambda i, *_: (0,) * t.ndim)
    return [whole(tables[n]) for n in names], [tables[n] for n in names]


def cost(flops, size):
    return pl.CostEstimate(flops=flops, bytes_accessed=size, transcendentals=0)


LIMIT = pltpu.CompilerParams(vmem_limit_bytes=48 * 2**20)


def filter_spectrum(filters, tables):
    count, r, a, m = filters.shape
    specs, operands = table_specs(tables, ("first", "turn", "forward"))
    return pl.pallas_call(
        filter_kernel,
        grid=(count,),
        out_shape=jax.ShapeDtypeStruct((count, r * HALF, 2 * m), jnp.float32),
        in_specs=specs + [pl.BlockSpec((None, r, a, m), lambda i: (i, 0, 0, 0))],
        out_specs=pl.BlockSpec((None, r * HALF, 2 * m), lambda i: (i, 0, 0)),
        cost_estimate=cost(10**9, 8 * filters.size),
        compiler_params=LIMIT,
    )(*operands, filters)


def input_grad_part(at_x, grad, filter_spec, tables):
    a, count, r, m = grad.shape
    names = ("first", "turn", "forward", "inverse", "last")
    specs, operands = table_specs(tables, names)
    spec_shape = (None, r * HALF, 2 * m)
    grid_spec = pltpu.PrefetchScalarGridSpec(
        num_scalar_prefetch=1,
        grid=(count,),
        in_specs=specs
        + [
            pl.BlockSpec((a, None, r, m), lambda i, at: (0, i, 0, 0)),
            pl.BlockSpec(spec_shape, lambda i, at: ((at[0] - i) & (count - 1), 0, 0)),
        ],
        out_specs=[
            pl.BlockSpec(spec_shape, lambda i, at: (i, 0, 0)),
            pl.BlockSpec((a, None, r, m), lambda i, at: (0, i, 0, 0)),
        ],
    )
    return pl.pallas_call(
        input_grad_kernel,
        grid_spec=grid_spec,
        out_shape=[
            jax.ShapeDtypeStruct((count, r * HALF, 2 * m), jnp.float32),
            jax.ShapeDtypeStruct((a, count, r, m), jnp.float32),
        ],
        cost_estimate=cost(2 * 10**9, 8 * grad.size),
        compiler_params=LIMIT,
    )(at_x, *operands, grad, filter_spec)


def filter_grad_part(at_x, tokens, grad_spec, tables):
    a, count, r, m = tokens.shape
    names = ("first", "turn", "forward", "inverse", "last_scaled")
    specs, operands = table_specs(tables, names)
    grid_spec = pltpu.PrefetchScalarGridSpec(
        num_scalar_prefetch=1,
        grid=(count,),
        in_specs=specs
        + [
            pl.BlockSpec((a, None, r, m), lambda i, at: (0, i, 0, 0)),
            pl.BlockSpec((None, r * HALF, 2 * m), lambda i, at: (i, 0, 0)),
        ],
        out_specs=pl.BlockSpec(
            (None, r, a, m), lambda i, at: ((i - at[0]) & (count - 1), 0, 0, 0)
        ),
    )
    return pl.pallas_call(
        filter_grad_kernel,
        grid_spec=grid_spec,
        out_shape=jax.ShapeDtypeStruct((count, r, a, m), jnp.float32),
        cost_estimate=cost(0, 0),
        compiler_params=LIMIT,
    )(at_x, *operands, tokens, grad_spec)


def pack_kernel(half, tokens, blocks):
    _, _, y, z, rows, _ = tokens.shape
    own, far, j = half[0], 1 - half[0], rows // 2
    for i in range(y):
        for k in range(z):
            near, other = tokens[:, own, i, k], tokens[:, far, i, z - 1 - k]
            blocks[i, k, 0] = jnp.concatenate([near[:, :j], other[:, :j]], axis=1)
            blocks[i, k, 1] = jnp.concatenate([near[:, j:], other[:, j:]], axis=1)


def unpack_kernel(half, blocks, tokens):
    _, _, y, z, rows, _ = tokens.shape
    own, far, j = half[0], 1 - half[0], rows // 2
    for i in range(y):
        for k in range(z):
            low, high = blocks[i, k, 0], blocks[i, k, 1]
            tokens[:, own, i, k] = jnp.concatenate([low[:, :j], high[:, :j]], axis=1)
            tokens[:, far, i, z - 1 - k] = jnp.concatenate([low[:, j:], high[:, j:]], axis=1)


def moving(kernel, half, array, shape):
    whole = pl.BlockSpec(memory_space=pltpu.VMEM)
    return pl.pallas_call(
        kernel,
        out_shape=jax.ShapeDtypeStruct(shape, jnp.float32),
        in_specs=[pl.BlockSpec(memory_space=pltpu.SMEM), whole],
        out_specs=whole,
        cost_estimate=cost(0, 8 * math.prod(shape)),
    )(half, array)


def shards(inputs, grad_out, filters):
    x, h, y, z, c = (lax.axis_size(a) for a in ("x", "zh", "y", "zl", "c"))
    _, channels, block = inputs.shape
    j = channels // (x * h * y * z * c)
    seq_length = filters.shape[1]
    rows = y * z * c
    tables = dft_tables(seq_length, 1.0 / math.sqrt(x * h * seq_length))
    half = lax.axis_index("zh").reshape(1).astype(jnp.int32)
    at_x = lax.axis_index("x").reshape(1).astype(jnp.int32)
    whole_shape = (x, h, y, z, c * j, INNER)

    def exchange(blocks):
        return lax.all_to_all(blocks, ("y", "zl", "c"), 0, 0, tiled=True)

    def facing(v):
        return lax.ppermute(v, ("zh", "zl"), [(i, h * z - 1 - i) for i in range(h * z)])

    def along_x(v, s):
        return lax.ppermute(v, "x", [(i, (i + s) % x) for i in range(x)])

    def to_owners(array):
        blocks = moving(pack_kernel, half, array.reshape(whole_shape), (y, z, c, x, h * j, INNER))
        return exchange(blocks.reshape(rows, x, h * j, INNER))

    grad = to_owners(grad_out)
    tokens = to_owners(inputs)

    filters = filters.reshape(j, rows, INNER)
    pair = jnp.concatenate([filters, facing(filters)])
    taps = jnp.stack([pair] + [along_x(pair, s) for s in range(1, x)])
    filter_spec = filter_spectrum(taps, tables)

    grad_spec, leaving = input_grad_part(at_x, grad, filter_spec, tables)
    returned = exchange(leaving)

    parts = filter_grad_part(at_x, tokens, grad_spec, tables)
    part = parts[0] + sum(along_x(parts[s], s) for s in range(1, x))
    filter_grad = part[:j] + facing(part[j:])

    blocks = returned.reshape(y, z, c, x, h * j, INNER)
    input_grad = moving(unpack_kernel, half, blocks, whole_shape)
    return (input_grad.reshape(1, channels, block), filter_grad.reshape(j, seq_length))


def solution(mesh):
    devices = mesh.devices.reshape(4, 2, 4, -1, 2)
    fine = Mesh(devices, ("x", "zh", "y", "zl", "c"))
    tokens = P(("x", "zh"), None, ("y", "zl", "c"))
    owners = P(("x", "zh", "y", "zl", "c"), None)
    return jax.shard_map(
        shards,
        mesh=fine,
        in_specs=(tokens, tokens, owners),
        out_specs=(tokens, owners),
        check_vma=False,
    )
```

```python
import math

import jax
import jax.numpy as jnp
import numpy as np
from jax import lax
from jax.experimental import pallas as pl
from jax.experimental.pallas import tpu as pltpu
from jax.sharding import Mesh
from jax.sharding import PartitionSpec as P

INNER = 128
HALF = 72


def three_parts(table, axis):
    high = np.asarray(table, np.float32).astype(jnp.bfloat16)
    low = (table - high.astype(np.float64)).astype(jnp.bfloat16)
    return jnp.asarray(np.concatenate([high, high, low], axis=axis))


def dft_tables(seq_length, norm):
    padded = 2 * seq_length
    outer = padded // INNER
    rows = seq_length // INNER
    freqs = outer // 2 + 1
    row, freq, inner = np.arange(rows), np.arange(freqs), np.arange(INNER)
    pad = ((0, HALF - freqs), (0, 0))
    angle = 2.0 * np.pi / outer * (freq[:, None] * row[None, :] % outer)
    cos_outer, sin_outer = np.pad(np.cos(angle), pad), np.pad(np.sin(angle), pad)
    weights = np.where((freq == 0) | (freq == freqs - 1), 1.0, 2.0)[:, None] / padded
    weights = np.pad(weights, pad)
    first = np.concatenate([cos_outer, -sin_outer], axis=0)
    last = np.concatenate([cos_outer * weights, -sin_outer * weights], axis=0).T
    angle = 2.0 * np.pi / INNER * (inner[:, None] * inner[None, :] % INNER)
    cos_inner, sin_inner = np.cos(angle), np.sin(angle)
    forward = np.block([[cos_inner, -sin_inner], [sin_inner, cos_inner]])
    inverse = np.block([[cos_inner, sin_inner], [-sin_inner, cos_inner]])
    angle = 2.0 * np.pi / padded * (freq[:, None] * inner[None, :] % padded)
    turn = np.stack([np.pad(np.cos(angle), pad), np.pad(np.sin(angle), pad)])
    left = dict(first=first, last=last, last_scaled=last * norm)
    right = dict(forward=forward, inverse=inverse)
    tables = {name: three_parts(t, 1) for name, t in left.items()}
    tables.update({name: three_parts(t, 0) for name, t in right.items()})
    tables["turn"] = jnp.asarray(turn, jnp.float32)
    return tables


def split(values):
    high = values.astype(jnp.bfloat16)
    return high, (values - high.astype(jnp.float32)).astype(jnp.bfloat16)


def dot(a, b):
    return jnp.dot(a, b, preferred_element_type=jnp.float32)


def forward_spectrum(wide, first, turn, forward):
    high, low = split(wide)
    outer = dot(first[...], jnp.concatenate([high, low, high], axis=0))
    cos, sin = turn[0], turn[1]
    turned = []
    for at in range(0, wide.shape[1], INNER):
        real, imag = outer[:HALF, at : at + INNER], outer[HALF:, at : at + INNER]
        turned.append(
            jnp.concatenate([real * cos + imag * sin, imag * cos - real * sin], axis=1)
        )
    high, low = split(jnp.concatenate(turned, axis=0))
    return dot(jnp.concatenate([high, low, high], axis=1), forward[...])


def correlate(spec, other):
    real, imag = spec[:, :INNER], spec[:, INNER:]
    other_real, other_imag = other[:, :INNER], other[:, INNER:]
    return jnp.concatenate(
        [real * other_real + imag * other_imag, imag * other_real - real * other_imag], axis=1
    )


def inverse_signal(spec, inverse, turn, last):
    high, low = split(spec)
    middle = dot(jnp.concatenate([high, low, high], axis=1), inverse[...])
    cos, sin = turn[0], turn[1]
    back = []
    for at in range(0, spec.shape[0], HALF):
        real, imag = middle[at : at + HALF, :INNER], middle[at : at + HALF, INNER:]
        back.append(
            jnp.concatenate([real * cos - imag * sin, imag * cos + real * sin], axis=0)
        )
    high, low = split(jnp.concatenate(back, axis=1))
    return dot(last[...], jnp.concatenate([high, low, high], axis=0))


def row(r, block):
    a, rows, _ = block.shape
    return pl.ds(r, a, stride=rows)


def rows_to_wide(block):
    a, rows, m = block.shape
    flat = block.reshape(a * rows, m)
    return jnp.concatenate([flat[row(r, block), :] for r in range(rows)], axis=1)


def filter_kernel(first, turn, forward, filters, spec):
    wide = jnp.concatenate([filters[r] for r in range(filters.shape[0])], axis=1)
    spec[...] = forward_spectrum(wide, first, turn, forward)


def input_grad_kernel(at, first, turn, forward, inverse, last, grad, filter_spec, spec, out):
    spec[...] = forward_spectrum(rows_to_wide(grad), first, turn, forward)
    wide = inverse_signal(correlate(spec[...], filter_spec[...]), inverse, turn, last)
    a, rows, m = out.shape
    flat = out.reshape(a * rows, m)
    for r in range(rows):
        flat[row(r, out), :] = wide[:, r * INNER : (r + 1) * INNER]


def filter_grad_kernel(at, first, turn, forward, inverse, last, tokens, grad_spec, out):
    spec = forward_spectrum(rows_to_wide(tokens), first, turn, forward)
    wide = inverse_signal(correlate(grad_spec[...], spec), inverse, turn, last)
    for r in range(out.shape[0]):
        out[r] = wide[:, r * INNER : (r + 1) * INNER]


def table_specs(tables, names):
    whole = lambda t: pl.BlockSpec(t.shape, lambda i, *_: (0,) * t.ndim)
    return [whole(tables[n]) for n in names], [tables[n] for n in names]


def cost(flops, size):
    return pl.CostEstimate(flops=flops, bytes_accessed=size, transcendentals=0)


LIMIT = pltpu.CompilerParams(vmem_limit_bytes=48 * 2**20)


def filter_spectrum(filters, tables):
    count, r, a, m = filters.shape
    specs, operands = table_specs(tables, ("first", "turn", "forward"))
    return pl.pallas_call(
        filter_kernel,
        grid=(count,),
        out_shape=jax.ShapeDtypeStruct((count, r * HALF, 2 * m), jnp.float32),
        in_specs=specs + [pl.BlockSpec((None, r, a, m), lambda i: (i, 0, 0, 0))],
        out_specs=pl.BlockSpec((None, r * HALF, 2 * m), lambda i: (i, 0, 0)),
        cost_estimate=cost(83 * 10**9, 8 * filters.size),
        compiler_params=LIMIT,
    )(*operands, filters)


def input_grad_part(at_x, both, filter_spec, tables):
    a, _, count, r, m = both.shape
    names = ("first", "turn", "forward", "inverse", "last")
    specs, operands = table_specs(tables, names)
    spec_shape = (None, r * HALF, 2 * m)
    grid_spec = pltpu.PrefetchScalarGridSpec(
        num_scalar_prefetch=1,
        grid=(count,),
        in_specs=specs
        + [
            pl.BlockSpec((a, None, None, r, m), lambda i, at: (0, 0, i, 0, 0)),
            pl.BlockSpec(spec_shape, lambda i, at: ((at[0] - i) & (count - 1), 0, 0)),
        ],
        out_specs=[
            pl.BlockSpec(spec_shape, lambda i, at: (i, 0, 0)),
            pl.BlockSpec((a, None, r, m), lambda i, at: (0, i, 0, 0)),
        ],
    )
    return pl.pallas_call(
        input_grad_kernel,
        grid_spec=grid_spec,
        out_shape=[
            jax.ShapeDtypeStruct((count, r * HALF, 2 * m), jnp.float32),
            jax.ShapeDtypeStruct((a, count, r, m), jnp.float32),
        ],
        cost_estimate=cost(2 * 10**9, 8 * both.size),
        compiler_params=LIMIT,
    )(at_x, *operands, both, filter_spec)


def filter_grad_part(at_x, both, grad_spec, tables):
    a, _, count, r, m = both.shape
    names = ("first", "turn", "forward", "inverse", "last_scaled")
    specs, operands = table_specs(tables, names)
    grid_spec = pltpu.PrefetchScalarGridSpec(
        num_scalar_prefetch=1,
        grid=(count,),
        in_specs=specs
        + [
            pl.BlockSpec((a, None, None, r, m), lambda i, at: (0, 1, i, 0, 0)),
            pl.BlockSpec((None, r * HALF, 2 * m), lambda i, at: (i, 0, 0)),
        ],
        out_specs=pl.BlockSpec(
            (None, r, a, m), lambda i, at: ((i - at[0]) & (count - 1), 0, 0, 0)
        ),
    )
    return pl.pallas_call(
        filter_grad_kernel,
        grid_spec=grid_spec,
        out_shape=jax.ShapeDtypeStruct((count, r, a, m), jnp.float32),
        cost_estimate=cost(0, 0),
        compiler_params=LIMIT,
    )(at_x, *operands, both, grad_spec)


def pack_kernel(half, grad, tokens, blocks):
    _, _, y, z, rows, _ = tokens.shape
    own, far, j = half[0], 1 - half[0], rows // 2
    for i in range(y):
        for k in range(z):
            for n, array in enumerate((grad, tokens)):
                near, other = array[:, own, i, k], array[:, far, i, z - 1 - k]
                blocks[i, k, 0, n] = jnp.concatenate([near[:, :j], other[:, :j]], axis=1)
                blocks[i, k, 1, n] = jnp.concatenate([near[:, j:], other[:, j:]], axis=1)


def unpack_kernel(half, blocks, tokens):
    _, _, y, z, rows, _ = tokens.shape
    own, far, j = half[0], 1 - half[0], rows // 2
    for i in range(y):
        for k in range(z):
            low, high = blocks[i, k, 0], blocks[i, k, 1]
            tokens[:, own, i, k] = jnp.concatenate([low[:, :j], high[:, :j]], axis=1)
            tokens[:, far, i, z - 1 - k] = jnp.concatenate([low[:, j:], high[:, j:]], axis=1)


def moving(kernel, half, arrays, shape):
    whole = pl.BlockSpec(memory_space=pltpu.VMEM)
    return pl.pallas_call(
        kernel,
        out_shape=jax.ShapeDtypeStruct(shape, jnp.float32),
        in_specs=[pl.BlockSpec(memory_space=pltpu.SMEM)] + [whole] * len(arrays),
        out_specs=whole,
        cost_estimate=cost(0, 8 * math.prod(shape)),
    )(half, *arrays)


def shards(inputs, grad_out, filters):
    x, h, y, z, c = (lax.axis_size(a) for a in ("x", "zh", "y", "zl", "c"))
    _, channels, block = inputs.shape
    j = channels // (x * h * y * z * c)
    seq_length = filters.shape[1]
    rows = y * z * c
    tables = dft_tables(seq_length, 1.0 / math.sqrt(x * h * seq_length))
    half = lax.axis_index("zh").reshape(1).astype(jnp.int32)
    at_x = lax.axis_index("x").reshape(1).astype(jnp.int32)
    whole_shape = (x, h, y, z, c * j, INNER)

    def exchange(blocks):
        return lax.all_to_all(blocks, ("y", "zl", "c"), 0, 0, tiled=True)

    def facing(v):
        return lax.ppermute(v, ("zh", "zl"), [(i, h * z - 1 - i) for i in range(h * z)])

    def along_x(v, s):
        return lax.ppermute(v, "x", [(i, (i + s) % x) for i in range(x)])

    both = moving(
        pack_kernel,
        half,
        [grad_out.reshape(whole_shape), inputs.reshape(whole_shape)],
        (y, z, c, 2, x, h * j, INNER),
    )
    both = exchange(both.reshape(rows, 2, x, h * j, INNER))

    pair = jnp.concatenate([filters, facing(filters)]).reshape(h * j, rows, INNER)
    taps = jnp.stack([pair] + [along_x(pair, s) for s in range(1, x)])
    filter_spec = filter_spectrum(taps, tables)

    grad_spec, leaving = input_grad_part(at_x, both, filter_spec, tables)
    returned = exchange(leaving)

    parts = filter_grad_part(at_x, both, grad_spec, tables)
    part = parts[0] + sum(along_x(parts[s], s) for s in range(1, x))
    filter_grad = part[:j] + facing(part[j:])

    blocks = returned.reshape(y, z, c, x, h * j, INNER)
    input_grad = moving(unpack_kernel, half, [blocks], whole_shape)
    return (input_grad.reshape(1, channels, block), filter_grad.reshape(j, seq_length))


def solution(mesh):
    devices = mesh.devices.reshape(4, 2, 4, -1, 2)
    fine = Mesh(devices, ("x", "zh", "y", "zl", "c"))
    tokens = P(("x", "zh"), None, ("y", "zl", "c"))
    owners = P(("x", "zh", "y", "zl", "c"), None)
    return jax.shard_map(
        shards,
        mesh=fine,
        in_specs=(tokens, tokens, owners),
        out_specs=(tokens, owners),
        check_vma=False,
    )
```

```python
import math

import jax
import jax.numpy as jnp
import numpy as np
from jax import lax
from jax.experimental import pallas as pl
from jax.experimental.pallas import tpu as pltpu
from jax.sharding import Mesh
from jax.sharding import PartitionSpec as P

INNER = 128
HALF = 72


def three_parts(table, axis):
    high = np.asarray(table, np.float32).astype(jnp.bfloat16)
    low = (table - high.astype(np.float64)).astype(jnp.bfloat16)
    return jnp.asarray(np.concatenate([high, high, low], axis=axis))


def dft_tables(seq_length, norm):
    padded = 2 * seq_length
    outer = padded // INNER
    rows = seq_length // INNER
    freqs = outer // 2 + 1
    row, freq, inner = np.arange(rows), np.arange(freqs), np.arange(INNER)
    pad = ((0, HALF - freqs), (0, 0))
    angle = 2.0 * np.pi / outer * (freq[:, None] * row[None, :] % outer)
    cos_outer, sin_outer = np.pad(np.cos(angle), pad), np.pad(np.sin(angle), pad)
    weights = np.where((freq == 0) | (freq == freqs - 1), 1.0, 2.0)[:, None] / padded
    weights = np.pad(weights, pad)
    first = np.concatenate([cos_outer, -sin_outer], axis=0)
    last = np.concatenate([cos_outer * weights, -sin_outer * weights], axis=0).T
    angle = 2.0 * np.pi / INNER * (inner[:, None] * inner[None, :] % INNER)
    cos_inner, sin_inner = np.cos(angle), np.sin(angle)
    forward = np.block([[cos_inner, -sin_inner], [sin_inner, cos_inner]])
    inverse = np.block([[cos_inner, sin_inner], [-sin_inner, cos_inner]])
    angle = 2.0 * np.pi / padded * (freq[:, None] * inner[None, :] % padded)
    turn = np.stack([np.pad(np.cos(angle), pad), np.pad(np.sin(angle), pad)])
    left = dict(first=first, last=last, last_scaled=last * norm)
    right = dict(forward=forward, inverse=inverse)
    tables = {name: three_parts(t, 1) for name, t in left.items()}
    tables.update({name: three_parts(t, 0) for name, t in right.items()})
    tables["turn"] = jnp.asarray(turn, jnp.float32)
    return tables


def split(values):
    high = values.astype(jnp.bfloat16)
    return high, (values - high.astype(jnp.float32)).astype(jnp.bfloat16)


def dot(a, b):
    return jnp.dot(a, b, preferred_element_type=jnp.float32)


def forward_spectrum(wide, first, turn, forward):
    high, low = split(wide)
    outer = dot(first[...], jnp.concatenate([high, low, high], axis=0))
    cos, sin = turn[0], turn[1]
    turned = []
    for at in range(0, wide.shape[1], INNER):
        real, imag = outer[:HALF, at : at + INNER], outer[HALF:, at : at + INNER]
        turned.append(
            jnp.concatenate([real * cos + imag * sin, imag * cos - real * sin], axis=1)
        )
    high, low = split(jnp.concatenate(turned, axis=0))
    return dot(jnp.concatenate([high, low, high], axis=1), forward[...])


def correlate(spec, other):
    real, imag = spec[:, :INNER], spec[:, INNER:]
    other_real, other_imag = other[:, :INNER], other[:, INNER:]
    return jnp.concatenate(
        [real * other_real + imag * other_imag, imag * other_real - real * other_imag], axis=1
    )


def inverse_signal(spec, inverse, turn, last):
    high, low = split(spec)
    middle = dot(jnp.concatenate([high, low, high], axis=1), inverse[...])
    cos, sin = turn[0], turn[1]
    back = []
    for at in range(0, spec.shape[0], HALF):
        real, imag = middle[at : at + HALF, :INNER], middle[at : at + HALF, INNER:]
        back.append(
            jnp.concatenate([real * cos - imag * sin, imag * cos + real * sin], axis=0)
        )
    high, low = split(jnp.concatenate(back, axis=1))
    return dot(last[...], jnp.concatenate([high, low, high], axis=0))


def row(r, block):
    a, rows, _ = block.shape
    return pl.ds(r, a, stride=rows)


def rows_to_wide(block):
    a, rows, m = block.shape
    flat = block.reshape(a * rows, m)
    return jnp.concatenate([flat[row(r, block), :] for r in range(rows)], axis=1)


def filter_kernel(first, turn, forward, filters, spec):
    wide = jnp.concatenate([filters[r] for r in range(filters.shape[0])], axis=1)
    spec[...] = forward_spectrum(wide, first, turn, forward)


def input_grad_kernel(at, first, turn, forward, inverse, last, grad, filter_spec, spec, out):
    spec[...] = forward_spectrum(rows_to_wide(grad), first, turn, forward)
    wide = inverse_signal(correlate(spec[...], filter_spec[...]), inverse, turn, last)
    a, rows, m = out.shape
    flat = out.reshape(a * rows, m)
    for r in range(rows):
        flat[row(r, out), :] = wide[:, r * INNER : (r + 1) * INNER]


def filter_grad_kernel(at, first, turn, forward, inverse, last, tokens, grad_spec, out):
    spec = forward_spectrum(rows_to_wide(tokens), first, turn, forward)
    wide = inverse_signal(correlate(grad_spec[...], spec), inverse, turn, last)
    for r in range(out.shape[0]):
        out[r] = wide[:, r * INNER : (r + 1) * INNER]


def table_specs(tables, names):
    whole = lambda t: pl.BlockSpec(t.shape, lambda i, *_: (0,) * t.ndim)
    return [whole(tables[n]) for n in names], [tables[n] for n in names]


def cost(flops, size):
    return pl.CostEstimate(flops=flops, bytes_accessed=size, transcendentals=0)


LIMIT = pltpu.CompilerParams(vmem_limit_bytes=48 * 2**20)


def filter_spectrum(filters, tables):
    count, r, a, m = filters.shape
    specs, operands = table_specs(tables, ("first", "turn", "forward"))
    return pl.pallas_call(
        filter_kernel,
        grid=(count,),
        out_shape=jax.ShapeDtypeStruct((count, r * HALF, 2 * m), jnp.float32),
        in_specs=specs + [pl.BlockSpec((None, r, a, m), lambda i: (i, 0, 0, 0))],
        out_specs=pl.BlockSpec((None, r * HALF, 2 * m), lambda i: (i, 0, 0)),
        cost_estimate=cost(83 * 10**9, 8 * filters.size),
        compiler_params=LIMIT,
    )(*operands, filters)


def input_grad_part(at_x, both, filter_spec, tables):
    a, _, count, r, m = both.shape
    names = ("first", "turn", "forward", "inverse", "last")
    specs, operands = table_specs(tables, names)
    spec_shape = (None, r * HALF, 2 * m)
    grid_spec = pltpu.PrefetchScalarGridSpec(
        num_scalar_prefetch=1,
        grid=(count,),
        in_specs=specs
        + [
            pl.BlockSpec((a, None, None, r, m), lambda i, at: (0, 0, i, 0, 0)),
            pl.BlockSpec(spec_shape, lambda i, at: ((at[0] - i) & (count - 1), 0, 0)),
        ],
        out_specs=[
            pl.BlockSpec(spec_shape, lambda i, at: (i, 0, 0)),
            pl.BlockSpec((a, None, r, m), lambda i, at: (0, i, 0, 0)),
        ],
    )
    return pl.pallas_call(
        input_grad_kernel,
        grid_spec=grid_spec,
        out_shape=[
            jax.ShapeDtypeStruct((count, r * HALF, 2 * m), jnp.float32),
            jax.ShapeDtypeStruct((a, count, r, m), jnp.float32),
        ],
        cost_estimate=cost(2 * 10**9, 8 * both.size),
        compiler_params=LIMIT,
    )(at_x, *operands, both, filter_spec)


def filter_grad_part(at_x, both, grad_spec, tables):
    a, _, count, r, m = both.shape
    names = ("first", "turn", "forward", "inverse", "last_scaled")
    specs, operands = table_specs(tables, names)
    grid_spec = pltpu.PrefetchScalarGridSpec(
        num_scalar_prefetch=1,
        grid=(count,),
        in_specs=specs
        + [
            pl.BlockSpec((a, None, None, r, m), lambda i, at: (0, 1, i, 0, 0)),
            pl.BlockSpec((None, r * HALF, 2 * m), lambda i, at: (i, 0, 0)),
        ],
        out_specs=pl.BlockSpec(
            (None, r, a, m), lambda i, at: ((i - at[0]) & (count - 1), 0, 0, 0)
        ),
    )
    return pl.pallas_call(
        filter_grad_kernel,
        grid_spec=grid_spec,
        out_shape=jax.ShapeDtypeStruct((count, r, a, m), jnp.float32),
        cost_estimate=cost(0, 0),
        compiler_params=LIMIT,
    )(at_x, *operands, both, grad_spec)


def pack_kernel(half, grad, tokens, blocks):
    _, _, y, z, rows, _ = tokens.shape
    own, far, j = half[0], 1 - half[0], rows // 2
    for i in range(y):
        for k in range(z):
            for n, array in enumerate((grad, tokens)):
                near, other = array[:, own, i, k], array[:, far, i, z - 1 - k]
                blocks[i, k, 0, n] = jnp.concatenate([near[:, :j], other[:, :j]], axis=1)
                blocks[i, k, 1, n] = jnp.concatenate([near[:, j:], other[:, j:]], axis=1)


def unpack_kernel(half, blocks, tokens):
    _, _, y, z, rows, _ = tokens.shape
    own, far, j = half[0], 1 - half[0], rows // 2
    for i in range(y):
        for k in range(z):
            low, high = blocks[i, k, 0], blocks[i, k, 1]
            tokens[:, own, i, k] = jnp.concatenate([low[:, :j], high[:, :j]], axis=1)
            tokens[:, far, i, z - 1 - k] = jnp.concatenate([low[:, j:], high[:, j:]], axis=1)


def moving(kernel, half, arrays, shape):
    whole = pl.BlockSpec(memory_space=pltpu.VMEM)
    return pl.pallas_call(
        kernel,
        out_shape=jax.ShapeDtypeStruct(shape, jnp.float32),
        in_specs=[pl.BlockSpec(memory_space=pltpu.SMEM)] + [whole] * len(arrays),
        out_specs=whole,
        cost_estimate=cost(0, 8 * math.prod(shape)),
    )(half, *arrays)


def shards(inputs, grad_out, filters):
    x, h, y, z, c = (lax.axis_size(a) for a in ("x", "zh", "y", "zl", "c"))
    _, channels, block = inputs.shape
    j = channels // (x * h * y * z * c)
    seq_length = filters.shape[1]
    rows = y * z * c
    tables = dft_tables(seq_length, 1.0 / math.sqrt(x * h * seq_length))
    half = lax.axis_index("zh").reshape(1).astype(jnp.int32)
    at_x = lax.axis_index("x").reshape(1).astype(jnp.int32)
    whole_shape = (x, h, y, z, c * j, INNER)

    def exchange(blocks):
        return lax.all_to_all(blocks, ("y", "zl", "c"), 0, 0, tiled=True)

    def facing(v):
        return lax.ppermute(v, ("zh", "zl"), [(i, h * z - 1 - i) for i in range(h * z)])

    def along_x(v, s):
        return lax.ppermute(v, "x", [(i, (i + s) % x) for i in range(x)])

    both = moving(
        pack_kernel,
        half,
        [grad_out.reshape(whole_shape), inputs.reshape(whole_shape)],
        (y, z, c, 2, x, h * j, INNER),
    )
    both, filters = lax.optimization_barrier((both, filters))
    both = exchange(both.reshape(rows, 2, x, h * j, INNER))

    pair = jnp.concatenate([filters, facing(filters)]).reshape(h * j, rows, INNER)
    taps = jnp.stack([pair] + [along_x(pair, s) for s in range(1, x)])
    filter_spec = filter_spectrum(taps, tables)

    grad_spec, leaving = input_grad_part(at_x, both, filter_spec, tables)
    returned = exchange(leaving)

    parts = filter_grad_part(at_x, both, grad_spec, tables)
    part = parts[0] + sum(along_x(parts[s], s) for s in range(1, x))
    filter_grad = part[:j] + facing(part[j:])

    blocks = returned.reshape(y, z, c, x, h * j, INNER)
    input_grad = moving(unpack_kernel, half, [blocks], whole_shape)
    return (input_grad.reshape(1, channels, block), filter_grad.reshape(j, seq_length))


def solution(mesh):
    devices = mesh.devices.reshape(4, 2, 4, -1, 2)
    fine = Mesh(devices, ("x", "zh", "y", "zl", "c"))
    tokens = P(("x", "zh"), None, ("y", "zl", "c"))
    owners = P(("x", "zh", "y", "zl", "c"), None)
    return jax.shard_map(
        shards,
        mesh=fine,
        in_specs=(tokens, tokens, owners),
        out_specs=(tokens, owners),
        check_vma=False,
    )
```

```python
import math

import jax
import jax.numpy as jnp
import numpy as np
from jax import lax
from jax.experimental import pallas as pl
from jax.experimental.pallas import tpu as pltpu
from jax.sharding import Mesh
from jax.sharding import PartitionSpec as P

INNER = 128
HALF = 72


def three_parts(table, axis):
    high = np.asarray(table, np.float32).astype(jnp.bfloat16)
    low = (table - high.astype(np.float64)).astype(jnp.bfloat16)
    return jnp.asarray(np.concatenate([high, high, low], axis=axis))


def dft_tables(seq_length, norm):
    padded = 2 * seq_length
    outer = padded // INNER
    rows = seq_length // INNER
    freqs = outer // 2 + 1
    row, freq, inner = np.arange(rows), np.arange(freqs), np.arange(INNER)
    pad = ((0, HALF - freqs), (0, 0))
    angle = 2.0 * np.pi / outer * (freq[:, None] * row[None, :] % outer)
    cos_outer, sin_outer = np.pad(np.cos(angle), pad), np.pad(np.sin(angle), pad)
    weights = np.where((freq == 0) | (freq == freqs - 1), 1.0, 2.0)[:, None] / padded
    weights = np.pad(weights, pad)
    first = np.concatenate([cos_outer, -sin_outer], axis=0)
    last = np.concatenate([cos_outer * weights, -sin_outer * weights], axis=0).T
    angle = 2.0 * np.pi / INNER * (inner[:, None] * inner[None, :] % INNER)
    cos_inner, sin_inner = np.cos(angle), np.sin(angle)
    forward = np.block([[cos_inner, -sin_inner], [sin_inner, cos_inner]])
    inverse = np.block([[cos_inner, sin_inner], [-sin_inner, cos_inner]])
    angle = 2.0 * np.pi / padded * (freq[:, None] * inner[None, :] % padded)
    turn = np.stack([np.pad(np.cos(angle), pad), np.pad(np.sin(angle), pad)])
    left = dict(first=first, last=last, last_scaled=last * norm)
    right = dict(forward=forward, inverse=inverse)
    tables = {name: three_parts(t, 1) for name, t in left.items()}
    tables.update({name: three_parts(t, 0) for name, t in right.items()})
    tables["turn"] = jnp.asarray(turn, jnp.float32)
    return tables


def split(values):
    high = values.astype(jnp.bfloat16)
    return high, (values - high.astype(jnp.float32)).astype(jnp.bfloat16)


def dot(a, b):
    return jnp.dot(a, b, preferred_element_type=jnp.float32)


def forward_spectrum(wide, first, turn, forward):
    high, low = split(wide)
    outer = dot(first[...], jnp.concatenate([high, low, high], axis=0))
    cos, sin = turn[0], turn[1]
    turned = []
    for at in range(0, wide.shape[1], INNER):
        real, imag = outer[:HALF, at : at + INNER], outer[HALF:, at : at + INNER]
        turned.append(
            jnp.concatenate([real * cos + imag * sin, imag * cos - real * sin], axis=1)
        )
    high, low = split(jnp.concatenate(turned, axis=0))
    return dot(jnp.concatenate([high, low, high], axis=1), forward[...])


def correlate(spec, other):
    real, imag = spec[:, :INNER], spec[:, INNER:]
    other_real, other_imag = other[:, :INNER], other[:, INNER:]
    return jnp.concatenate(
        [real * other_real + imag * other_imag, imag * other_real - real * other_imag], axis=1
    )


def inverse_signal(spec, inverse, turn, last):
    high, low = split(spec)
    middle = dot(jnp.concatenate([high, low, high], axis=1), inverse[...])
    cos, sin = turn[0], turn[1]
    back = []
    for at in range(0, spec.shape[0], HALF):
        real, imag = middle[at : at + HALF, :INNER], middle[at : at + HALF, INNER:]
        back.append(
            jnp.concatenate([real * cos - imag * sin, imag * cos + real * sin], axis=0)
        )
    high, low = split(jnp.concatenate(back, axis=1))
    return dot(last[...], jnp.concatenate([high, low, high], axis=0))


def row(r, block):
    a, rows, _ = block.shape
    return pl.ds(r, a, stride=rows)


def rows_to_wide(block):
    a, rows, m = block.shape
    flat = block.reshape(a * rows, m)
    return jnp.concatenate([flat[row(r, block), :] for r in range(rows)], axis=1)


def filter_kernel(at, first, turn, forward, filters, spec):
    wide = jnp.concatenate([filters[r] for r in range(filters.shape[0])], axis=1)
    spec[...] = forward_spectrum(wide, first, turn, forward)


def input_grad_kernel(first, turn, forward, inverse, last, grad, filter_spec, spec, out):
    spec[...] = forward_spectrum(rows_to_wide(grad), first, turn, forward)
    wide = inverse_signal(correlate(spec[...], filter_spec[...]), inverse, turn, last)
    a, rows, m = out.shape
    flat = out.reshape(a * rows, m)
    for r in range(rows):
        flat[row(r, out), :] = wide[:, r * INNER : (r + 1) * INNER]


def filter_grad_kernel(first, turn, forward, inverse, last, tokens, grad_spec, out, total):
    spec = forward_spectrum(rows_to_wide(tokens), first, turn, forward)
    share = correlate(grad_spec[...], spec)
    seq = pl.program_id(1)

    @pl.when(seq == 0)
    def _():
        total[...] = share

    @pl.when(seq > 0)
    def _():
        total[...] += share

    @pl.when(seq == pl.num_programs(1) - 1)
    def _():
        wide = inverse_signal(total[...], inverse, turn, last)
        for r in range(out.shape[0]):
            out[r] = wide[:, r * INNER : (r + 1) * INNER]


def table_specs(tables, names):
    whole = lambda t: pl.BlockSpec(t.shape, lambda *_: (0,) * t.ndim)
    return [whole(tables[n]) for n in names], [tables[n] for n in names]


def cost(flops, size):
    return pl.CostEstimate(flops=flops, bytes_accessed=size, transcendentals=0)


LIMIT = pltpu.CompilerParams(vmem_limit_bytes=48 * 2**20)


def filter_spectrum(at_x, filters, tables):
    count, r, a, m = filters.shape
    specs, operands = table_specs(tables, ("first", "turn", "forward"))
    grid_spec = pltpu.PrefetchScalarGridSpec(
        num_scalar_prefetch=1,
        grid=(count,),
        in_specs=specs + [pl.BlockSpec((None, r, a, m), lambda i, at: (i, 0, 0, 0))],
        out_specs=pl.BlockSpec(
            (None, r * HALF, 2 * m), lambda i, at: ((at[0] - i) & (count - 1), 0, 0)
        ),
    )
    return pl.pallas_call(
        filter_kernel,
        grid_spec=grid_spec,
        out_shape=jax.ShapeDtypeStruct((count, r * HALF, 2 * m), jnp.float32),
        cost_estimate=cost(10**9, 8 * filters.size),
        compiler_params=LIMIT,
    )(at_x, *operands, filters)


def input_grad_part(both, filter_spec, tables):
    seqs, a, _, pairs, r, m = both.shape
    names = ("first", "turn", "forward", "inverse", "last")
    specs, operands = table_specs(tables, names)
    spec_shape = (None, r * HALF, 2 * m)
    return pl.pallas_call(
        input_grad_kernel,
        grid=(pairs, seqs),
        in_specs=specs
        + [
            pl.BlockSpec((None, a, None, None, r, m), lambda p, q: (q, 0, 0, p, 0, 0)),
            pl.BlockSpec(spec_shape, lambda p, q: (p, 0, 0)),
        ],
        out_specs=[
            pl.BlockSpec((None, *spec_shape), lambda p, q: (q, p, 0, 0)),
            pl.BlockSpec((None, a, None, r, m), lambda p, q: (q, 0, p, 0, 0)),
        ],
        out_shape=[
            jax.ShapeDtypeStruct((seqs, pairs, r * HALF, 2 * m), jnp.float32),
            jax.ShapeDtypeStruct((seqs, a, pairs, r, m), jnp.float32),
        ],
        cost_estimate=cost(2 * 10**9, 8 * both.size),
        compiler_params=LIMIT,
    )(*operands, both, filter_spec)


def filter_grad_part(both, grad_spec, tables):
    seqs, a, _, pairs, r, m = both.shape
    names = ("first", "turn", "forward", "inverse", "last_scaled")
    specs, operands = table_specs(tables, names)
    return pl.pallas_call(
        filter_grad_kernel,
        grid=(pairs, seqs),
        in_specs=specs
        + [
            pl.BlockSpec((None, a, None, None, r, m), lambda p, q: (q, 0, 1, p, 0, 0)),
            pl.BlockSpec((None, None, r * HALF, 2 * m), lambda p, q: (q, p, 0, 0)),
        ],
        out_specs=pl.BlockSpec((None, r, a, m), lambda p, q: (p, 0, 0, 0)),
        out_shape=jax.ShapeDtypeStruct((pairs, r, a, m), jnp.float32),
        scratch_shapes=[pltpu.VMEM((r * HALF, 2 * m), jnp.float32)],
        cost_estimate=cost(0, 0),
        compiler_params=LIMIT,
    )(*operands, both, grad_spec)


def pack_kernel(grad, tokens, blocks):
    x, h, y, z, rows, lanes = tokens.shape
    j = rows // 2
    for g in range(h):
        for i in range(y):
            for k in range(z):
                for n, array in enumerate((grad, tokens)):
                    tiles = array[:, g, i, k].reshape(x // 2, 2, rows, lanes)
                    low, high = tiles[:, 0], tiles[:, 1]
                    blocks[g, i, k, 0, n] = jnp.concatenate([low[:, :j], high[:, :j]], axis=1)
                    blocks[g, i, k, 1, n] = jnp.concatenate([low[:, j:], high[:, j:]], axis=1)


def unpack_kernel(blocks, tokens):
    x, h, y, z, rows, lanes = tokens.shape
    j = rows // 2
    for g in range(h):
        for i in range(y):
            for k in range(z):
                low, high = blocks[g, i, k, 0], blocks[g, i, k, 1]
                even = jnp.concatenate([low[:, :j], high[:, :j]], axis=1)
                odd = jnp.concatenate([low[:, j:], high[:, j:]], axis=1)
                tokens[:, g, i, k] = jnp.stack([even, odd], axis=1).reshape(x, rows, lanes)


def moving(kernel, arrays, shape):
    whole = pl.BlockSpec(memory_space=pltpu.VMEM)
    return pl.pallas_call(
        kernel,
        out_shape=jax.ShapeDtypeStruct(shape, jnp.float32),
        in_specs=[whole] * len(arrays),
        out_specs=whole,
        cost_estimate=cost(0, 8 * math.prod(shape)),
    )(*arrays)


def shards(inputs, grad_out, filters):
    x, h, y, z, c = (lax.axis_size(a) for a in ("x", "zh", "y", "zl", "c"))
    _, channels, block = inputs.shape
    j = channels // (x * h * y * z * c)
    seq_length = filters.shape[1]
    rows = y * z * c
    pairs = x // 2
    tables = dft_tables(seq_length, 1.0 / math.sqrt(x * h * seq_length))
    at_x = lax.axis_index("x").reshape(1).astype(jnp.int32)
    whole_shape = (x, h, y, z, c * j, INNER)

    def exchange(blocks):
        return lax.all_to_all(blocks, ("zh", "y", "zl", "c"), 0, 0, tiled=True)

    def along_x(v, s):
        return lax.ppermute(v, "x", [(i, (i + s) % x) for i in range(x)])

    both = moving(
        pack_kernel,
        [grad_out.reshape(whole_shape), inputs.reshape(whole_shape)],
        (h, y, z, c, 2, pairs, 2 * j, INNER),
    )
    both = exchange(both.reshape(h * rows, 2, pairs, 2 * j, INNER))
    both = both.reshape(h, rows, 2, pairs, 2 * j, INNER)

    own = filters.reshape(j, rows, INNER)
    taps = jnp.stack([own] + [along_x(own, s) for s in range(1, x)])
    filter_spec = filter_spectrum(at_x, taps, tables).reshape(pairs, 2 * j * HALF, 2 * INNER)

    grad_spec, leaving = input_grad_part(both, filter_spec, tables)
    returned = exchange(leaving.reshape(h * rows, pairs, 2 * j, INNER))

    parts = filter_grad_part(both, grad_spec, tables).reshape(x, j, rows, INNER)
    share = [
        lax.dynamic_index_in_dim(parts, (at_x[0] + s) % x, 0, keepdims=False) for s in range(x)
    ]
    filter_grad = share[0] + sum(along_x(share[s], s) for s in range(1, x))

    blocks = returned.reshape(h, y, z, c, pairs, 2 * j, INNER)
    input_grad = moving(unpack_kernel, [blocks], whole_shape)
    return (input_grad.reshape(1, channels, block), filter_grad.reshape(j, seq_length))


def solution(mesh):
    devices = mesh.devices.reshape(4, 2, 4, -1, 2)
    fine = Mesh(devices, ("x", "zh", "y", "zl", "c"))
    tokens = P(("x", "zh"), None, ("y", "zl", "c"))
    owners = P(("x", "zh", "y", "zl", "c"), None)
    return jax.shard_map(
        shards,
        mesh=fine,
        in_specs=(tokens, tokens, owners),
        out_specs=(tokens, owners),
        check_vma=False,
    )
```

```python
import math

import jax
import jax.numpy as jnp
import numpy as np
from jax import lax
from jax.experimental import pallas as pl
from jax.experimental.pallas import tpu as pltpu
from jax.sharding import Mesh
from jax.sharding import PartitionSpec as P

INNER = 128
HALF = 72


def three_parts(table, axis):
    high = np.asarray(table, np.float32).astype(jnp.bfloat16)
    low = (table - high.astype(np.float64)).astype(jnp.bfloat16)
    return jnp.asarray(np.concatenate([high, high, low], axis=axis))


def dft_tables(seq_length, norm):
    padded = 2 * seq_length
    outer = padded // INNER
    rows = seq_length // INNER
    freqs = outer // 2 + 1
    row, freq, inner = np.arange(rows), np.arange(freqs), np.arange(INNER)
    pad = ((0, HALF - freqs), (0, 0))
    angle = 2.0 * np.pi / outer * (freq[:, None] * row[None, :] % outer)
    cos_outer, sin_outer = np.pad(np.cos(angle), pad), np.pad(np.sin(angle), pad)
    weights = np.where((freq == 0) | (freq == freqs - 1), 1.0, 2.0)[:, None] / padded
    weights = np.pad(weights, pad)
    first = np.concatenate([cos_outer, -sin_outer], axis=0)
    last = np.concatenate([cos_outer * weights, -sin_outer * weights], axis=0).T
    angle = 2.0 * np.pi / INNER * (inner[:, None] * inner[None, :] % INNER)
    cos_inner, sin_inner = np.cos(angle), np.sin(angle)
    forward = np.block([[cos_inner, -sin_inner], [sin_inner, cos_inner]])
    inverse = np.block([[cos_inner, sin_inner], [-sin_inner, cos_inner]])
    angle = 2.0 * np.pi / padded * (freq[:, None] * inner[None, :] % padded)
    turn = np.stack([np.pad(np.cos(angle), pad), np.pad(np.sin(angle), pad)])
    left = dict(first=first, last=last, last_scaled=last * norm)
    right = dict(forward=forward, inverse=inverse)
    tables = {name: three_parts(t, 1) for name, t in left.items()}
    tables.update({name: three_parts(t, 0) for name, t in right.items()})
    tables["turn"] = jnp.asarray(turn, jnp.float32)
    return tables


def split(values):
    high = values.astype(jnp.bfloat16)
    return high, (values - high.astype(jnp.float32)).astype(jnp.bfloat16)


def dot(a, b):
    return jnp.dot(a, b, preferred_element_type=jnp.float32)


def forward_spectrum(wide, first, turn, forward):
    high, low = split(wide)
    outer = dot(first[...], jnp.concatenate([high, low, high], axis=0))
    cos, sin = turn[0], turn[1]
    turned = []
    for at in range(0, wide.shape[1], INNER):
        real, imag = outer[:HALF, at : at + INNER], outer[HALF:, at : at + INNER]
        turned.append(
            jnp.concatenate([real * cos + imag * sin, imag * cos - real * sin], axis=1)
        )
    high, low = split(jnp.concatenate(turned, axis=0))
    return dot(jnp.concatenate([high, low, high], axis=1), forward[...])


def correlate(spec, other):
    real, imag = spec[:, :INNER], spec[:, INNER:]
    other_real, other_imag = other[:, :INNER], other[:, INNER:]
    return jnp.concatenate(
        [real * other_real + imag * other_imag, imag * other_real - real * other_imag], axis=1
    )


def inverse_signal(spec, inverse, turn, last):
    high, low = split(spec)
    middle = dot(jnp.concatenate([high, low, high], axis=1), inverse[...])
    cos, sin = turn[0], turn[1]
    back = []
    for at in range(0, spec.shape[0], HALF):
        real, imag = middle[at : at + HALF, :INNER], middle[at : at + HALF, INNER:]
        back.append(
            jnp.concatenate([real * cos - imag * sin, imag * cos + real * sin], axis=0)
        )
    high, low = split(jnp.concatenate(back, axis=1))
    return dot(last[...], jnp.concatenate([high, low, high], axis=0))


def row(r, block):
    a, rows, _ = block.shape
    return pl.ds(r, a, stride=rows)


def rows_to_wide(block):
    a, rows, m = block.shape
    flat = block.reshape(a * rows, m)
    return jnp.concatenate([flat[row(r, block), :] for r in range(rows)], axis=1)


def filter_kernel(first, turn, forward, filters, spec):
    wide = jnp.concatenate([filters[r] for r in range(filters.shape[0])], axis=1)
    spec[...] = forward_spectrum(wide, first, turn, forward)


def input_grad_kernel(at, first, turn, forward, inverse, last, grad, filter_spec, spec, out):
    spec[...] = forward_spectrum(rows_to_wide(grad), first, turn, forward)
    wide = inverse_signal(correlate(spec[...], filter_spec[...]), inverse, turn, last)
    a, rows, m = out.shape
    flat = out.reshape(a * rows, m)
    for r in range(rows):
        flat[row(r, out), :] = wide[:, r * INNER : (r + 1) * INNER]


def filter_grad_kernel(at, first, turn, forward, inverse, last, tokens, grad_spec, out):
    spec = forward_spectrum(rows_to_wide(tokens), first, turn, forward)
    wide = inverse_signal(correlate(grad_spec[...], spec), inverse, turn, last)
    for r in range(out.shape[0]):
        out[r] = wide[:, r * INNER : (r + 1) * INNER]


def table_specs(tables, names):
    whole = lambda t: pl.BlockSpec(t.shape, lambda i, *_: (0,) * t.ndim)
    return [whole(tables[n]) for n in names], [tables[n] for n in names]


def cost(flops, size):
    return pl.CostEstimate(flops=flops, bytes_accessed=size, transcendentals=0)


LIMIT = pltpu.CompilerParams(vmem_limit_bytes=48 * 2**20)


def filter_spectrum(filters, tables):
    count, r, a, m = filters.shape
    specs, operands = table_specs(tables, ("first", "turn", "forward"))
    return pl.pallas_call(
        filter_kernel,
        grid=(count,),
        out_shape=jax.ShapeDtypeStruct((count, r * HALF, 2 * m), jnp.float32),
        in_specs=specs + [pl.BlockSpec((None, r, a, m), lambda i: (i, 0, 0, 0))],
        out_specs=pl.BlockSpec((None, r * HALF, 2 * m), lambda i: (i, 0, 0)),
        cost_estimate=cost(10**9, 8 * filters.size),
        compiler_params=LIMIT,
    )(*operands, filters)


def input_grad_part(at_x, both, filter_spec, tables):
    a, _, count, r, m = both.shape
    names = ("first", "turn", "forward", "inverse", "last")
    specs, operands = table_specs(tables, names)
    spec_shape = (None, r * HALF, 2 * m)
    grid_spec = pltpu.PrefetchScalarGridSpec(
        num_scalar_prefetch=1,
        grid=(count,),
        in_specs=specs
        + [
            pl.BlockSpec((a, None, None, r, m), lambda i, at: (0, 0, i, 0, 0)),
            pl.BlockSpec(spec_shape, lambda i, at: ((at[0] - i) & (count - 1), 0, 0)),
        ],
        out_specs=[
            pl.BlockSpec(spec_shape, lambda i, at: (i, 0, 0)),
            pl.BlockSpec((a, None, r, m), lambda i, at: (0, i, 0, 0)),
        ],
    )
    return pl.pallas_call(
        input_grad_kernel,
        grid_spec=grid_spec,
        out_shape=[
            jax.ShapeDtypeStruct((count, r * HALF, 2 * m), jnp.float32),
            jax.ShapeDtypeStruct((a, count, r, m), jnp.float32),
        ],
        cost_estimate=cost(2 * 10**9, 8 * both.size),
        compiler_params=LIMIT,
    )(at_x, *operands, both, filter_spec)


def filter_grad_part(at_x, both, grad_spec, tables):
    a, _, count, r, m = both.shape
    names = ("first", "turn", "forward", "inverse", "last_scaled")
    specs, operands = table_specs(tables, names)
    grid_spec = pltpu.PrefetchScalarGridSpec(
        num_scalar_prefetch=1,
        grid=(count,),
        in_specs=specs
        + [
            pl.BlockSpec((a, None, None, r, m), lambda i, at: (0, 1, i, 0, 0)),
            pl.BlockSpec((None, r * HALF, 2 * m), lambda i, at: (i, 0, 0)),
        ],
        out_specs=pl.BlockSpec(
            (None, r, a, m), lambda i, at: ((i - at[0]) & (count - 1), 0, 0, 0)
        ),
    )
    return pl.pallas_call(
        filter_grad_kernel,
        grid_spec=grid_spec,
        out_shape=jax.ShapeDtypeStruct((count, r, a, m), jnp.float32),
        cost_estimate=cost(0, 0),
        compiler_params=LIMIT,
    )(at_x, *operands, both, grad_spec)


def in_parts(incoming, work, outgoing):
    for copies in incoming:
        for copy in copies:
            copy.start()
    for i, copies in enumerate(incoming):
        for copy in copies:
            copy.wait()
        work(i)
        outgoing[i].start()
    for copy in outgoing:
        copy.wait()


def pack_kernel(half, grad, tokens, blocks, arrived, leaving, in_sems, out_sems):
    _, _, y, z, rows, _ = tokens.shape
    own, far, j = half[0], 1 - half[0], rows // 2
    arrays = (grad, tokens)
    incoming = [
        [
            pltpu.make_async_copy(array.at[:, :, i], arrived.at[i, n], in_sems.at[i, n])
            for n, array in enumerate(arrays)
        ]
        for i in range(y)
    ]
    outgoing = [
        pltpu.make_async_copy(leaving.at[i], blocks.at[i], out_sems.at[i]) for i in range(y)
    ]

    def work(i):
        for k in range(z):
            for n in range(len(arrays)):
                near, other = arrived[i, n, :, own, k], arrived[i, n, :, far, k ^ (z // 2)]
                leaving[i, k, 0, n] = jnp.concatenate([near[:, :j], other[:, :j]], axis=1)
                leaving[i, k, 1, n] = jnp.concatenate([near[:, j:], other[:, j:]], axis=1)

    in_parts(incoming, work, outgoing)


def unpack_kernel(half, blocks, tokens, arrived, leaving, in_sems, out_sems):
    y, z, _, _, rows, _ = blocks.shape
    own, far, j = half[0], 1 - half[0], rows // 2
    incoming = [
        [pltpu.make_async_copy(blocks.at[i], arrived.at[i], in_sems.at[i])] for i in range(y)
    ]
    outgoing = [
        pltpu.make_async_copy(leaving.at[i], tokens.at[:, :, i], out_sems.at[i])
        for i in range(y)
    ]

    def work(i):
        for k in range(z):
            low, high = arrived[i, k, 0], arrived[i, k, 1]
            leaving[i, :, own, k] = jnp.concatenate([low[:, :j], high[:, :j]], axis=1)
            leaving[i, :, far, k ^ (z // 2)] = jnp.concatenate([low[:, j:], high[:, j:]], axis=1)

    in_parts(incoming, work, outgoing)


def moving(kernel, half, arrays, shape, scratch, sems):
    anywhere = pl.BlockSpec(memory_space=pl.ANY)
    return pl.pallas_call(
        kernel,
        out_shape=jax.ShapeDtypeStruct(shape, jnp.float32),
        in_specs=[pl.BlockSpec(memory_space=pltpu.SMEM)] + [anywhere] * len(arrays),
        out_specs=anywhere,
        scratch_shapes=[pltpu.VMEM(v, jnp.float32) for v in scratch]
        + [pltpu.SemaphoreType.DMA(v) for v in sems],
        cost_estimate=cost(0, 8 * math.prod(shape)),
    )(half, *arrays)


def pack(half, grad, tokens):
    x, h, y, z, rows, lanes = grad.shape
    shape = (y, z, 2, 2, x, rows, lanes)
    scratch = [(y, 2, x, h, z, rows, lanes), shape]
    return moving(pack_kernel, half, [grad, tokens], shape, scratch, [(y, 2), (y,)])


def unpack(half, blocks, shape):
    x, h, y, z, rows, lanes = shape
    scratch = [blocks.shape, (y, x, h, z, rows, lanes)]
    return moving(unpack_kernel, half, [blocks], shape, scratch, [(y,), (y,)])


def shards(inputs, grad_out, filters):
    x, h, y, z, c = (lax.axis_size(a) for a in ("x", "zh", "y", "zl", "c"))
    _, channels, block = inputs.shape
    j = channels // (x * h * y * z * c)
    seq_length = filters.shape[1]
    rows = y * z * c
    tables = dft_tables(seq_length, 1.0 / math.sqrt(x * h * seq_length))
    half = lax.axis_index("zh").reshape(1).astype(jnp.int32)
    at_x = lax.axis_index("x").reshape(1).astype(jnp.int32)
    whole_shape = (x, h, y, z, c * j, INNER)

    def exchange(blocks):
        return lax.all_to_all(blocks, ("y", "zl", "c"), 0, 0, tiled=True)

    def facing(v):
        return lax.ppermute(v, ("zh", "zl"), [(i, i ^ z ^ (z // 2)) for i in range(h * z)])

    def along_x(v, s):
        return lax.ppermute(v, "x", [(i, (i + s) % x) for i in range(x)])

    both = pack(half, grad_out.reshape(whole_shape), inputs.reshape(whole_shape))
    both, filters = lax.optimization_barrier((both, filters))
    both = exchange(both.reshape(rows, 2, x, h * j, INNER))

    pair = jnp.concatenate([filters, facing(filters)]).reshape(h * j, rows, INNER)
    taps = jnp.stack([pair] + [along_x(pair, s) for s in range(1, x)])
    filter_spec = filter_spectrum(taps, tables)

    grad_spec, leaving = input_grad_part(at_x, both, filter_spec, tables)
    returned = exchange(leaving)

    parts = filter_grad_part(at_x, both, grad_spec, tables)
    part = parts[0] + sum(along_x(parts[s], s) for s in range(1, x))
    filter_grad = part[:j] + facing(part[j:])

    blocks = returned.reshape(y, z, c, x, h * j, INNER)
    input_grad = unpack(half, blocks, whole_shape)
    return (input_grad.reshape(1, channels, block), filter_grad.reshape(j, seq_length))


def solution(mesh):
    devices = mesh.devices.reshape(4, 2, 4, -1, 2)
    fine = Mesh(devices, ("x", "zh", "y", "zl", "c"))
    tokens = P(("x", "zh"), None, ("y", "zl", "c"))
    owners = P(("x", "zh", "y", "zl", "c"), None)
    return jax.shard_map(
        shards,
        mesh=fine,
        in_specs=(tokens, tokens, owners),
        out_specs=(tokens, owners),
        check_vma=False,
    )
```

```python
import math

import jax
import jax.numpy as jnp
import numpy as np
from jax import lax
from jax.experimental import pallas as pl
from jax.experimental.pallas import tpu as pltpu
from jax.sharding import Mesh
from jax.sharding import PartitionSpec as P

INNER = 128
HALF = 72


def three_parts(table, axis):
    high = np.asarray(table, np.float32).astype(jnp.bfloat16)
    low = (table - high.astype(np.float64)).astype(jnp.bfloat16)
    return jnp.asarray(np.concatenate([high, high, low], axis=axis))


def dft_tables(seq_length, norm):
    padded = 2 * seq_length
    outer = padded // INNER
    rows = seq_length // INNER
    freqs = outer // 2 + 1
    row, freq, inner = np.arange(rows), np.arange(freqs), np.arange(INNER)
    pad = ((0, HALF - freqs), (0, 0))
    angle = 2.0 * np.pi / outer * (freq[:, None] * row[None, :] % outer)
    cos_outer, sin_outer = np.pad(np.cos(angle), pad), np.pad(np.sin(angle), pad)
    weights = np.where((freq == 0) | (freq == freqs - 1), 1.0, 2.0)[:, None] / padded
    weights = np.pad(weights, pad)
    first = np.concatenate([cos_outer, -sin_outer], axis=0)
    last = np.concatenate([cos_outer * weights, -sin_outer * weights], axis=0).T
    angle = 2.0 * np.pi / INNER * (inner[:, None] * inner[None, :] % INNER)
    cos_inner, sin_inner = np.cos(angle), np.sin(angle)
    forward = np.block([[cos_inner, -sin_inner], [sin_inner, cos_inner]])
    inverse = np.block([[cos_inner, sin_inner], [-sin_inner, cos_inner]])
    angle = 2.0 * np.pi / padded * (freq[:, None] * inner[None, :] % padded)
    turn = np.stack([np.pad(np.cos(angle), pad), np.pad(np.sin(angle), pad)])
    left = dict(first=first, last=last, last_scaled=last * norm)
    right = dict(forward=forward, inverse=inverse)
    tables = {name: three_parts(t, 1) for name, t in left.items()}
    tables.update({name: three_parts(t, 0) for name, t in right.items()})
    tables["turn"] = jnp.asarray(turn, jnp.float32)
    return tables


def split(values):
    high = values.astype(jnp.bfloat16)
    return high, (values - high.astype(jnp.float32)).astype(jnp.bfloat16)


def dot(a, b):
    return jnp.dot(a, b, preferred_element_type=jnp.float32)


def forward_spectrum(wide, first, turn, forward):
    high, low = split(wide)
    outer = dot(first[...], jnp.concatenate([high, low, high], axis=0))
    cos, sin = turn[0], turn[1]
    turned = []
    for at in range(0, wide.shape[1], INNER):
        real, imag = outer[:HALF, at : at + INNER], outer[HALF:, at : at + INNER]
        turned.append(
            jnp.concatenate([real * cos + imag * sin, imag * cos - real * sin], axis=1)
        )
    high, low = split(jnp.concatenate(turned, axis=0))
    return dot(jnp.concatenate([high, low, high], axis=1), forward[...])


def correlate(spec, other):
    real, imag = spec[:, :INNER], spec[:, INNER:]
    other_real, other_imag = other[:, :INNER], other[:, INNER:]
    return jnp.concatenate(
        [real * other_real + imag * other_imag, imag * other_real - real * other_imag], axis=1
    )


def inverse_signal(spec, inverse, turn, last):
    high, low = split(spec)
    middle = dot(jnp.concatenate([high, low, high], axis=1), inverse[...])
    cos, sin = turn[0], turn[1]
    back = []
    for at in range(0, spec.shape[0], HALF):
        real, imag = middle[at : at + HALF, :INNER], middle[at : at + HALF, INNER:]
        back.append(
            jnp.concatenate([real * cos - imag * sin, imag * cos + real * sin], axis=0)
        )
    high, low = split(jnp.concatenate(back, axis=1))
    return dot(last[...], jnp.concatenate([high, low, high], axis=0))


def row(r, block):
    a, rows, _ = block.shape
    return pl.ds(r, a, stride=rows)


def rows_to_wide(block):
    a, rows, m = block.shape
    flat = block.reshape(a * rows, m)
    return jnp.concatenate([flat[row(r, block), :] for r in range(rows)], axis=1)


def filter_kernel(first, turn, forward, filters, spec):
    wide = jnp.concatenate([filters[r] for r in range(filters.shape[0])], axis=1)
    spec[...] = forward_spectrum(wide, first, turn, forward)


def input_grad_kernel(at, first, turn, forward, inverse, last, grad, filter_spec, spec, out):
    spec[...] = forward_spectrum(rows_to_wide(grad), first, turn, forward)
    wide = inverse_signal(correlate(spec[...], filter_spec[...]), inverse, turn, last)
    a, rows, m = out.shape
    flat = out.reshape(a * rows, m)
    for r in range(rows):
        flat[row(r, out), :] = wide[:, r * INNER : (r + 1) * INNER]


def filter_grad_kernel(at, first, turn, forward, inverse, last, tokens, grad_spec, out):
    spec = forward_spectrum(rows_to_wide(tokens), first, turn, forward)
    wide = inverse_signal(correlate(grad_spec[...], spec), inverse, turn, last)
    for r in range(out.shape[0]):
        out[r] = wide[:, r * INNER : (r + 1) * INNER]


def table_specs(tables, names):
    whole = lambda t: pl.BlockSpec(t.shape, lambda i, *_: (0,) * t.ndim)
    return [whole(tables[n]) for n in names], [tables[n] for n in names]


def cost(flops, size):
    return pl.CostEstimate(flops=flops, bytes_accessed=size, transcendentals=0)


LIMIT = pltpu.CompilerParams(vmem_limit_bytes=48 * 2**20)


def filter_spectrum(filters, tables):
    count, r, a, m = filters.shape
    specs, operands = table_specs(tables, ("first", "turn", "forward"))
    return pl.pallas_call(
        filter_kernel,
        grid=(count,),
        out_shape=jax.ShapeDtypeStruct((count, r * HALF, 2 * m), jnp.float32),
        in_specs=specs + [pl.BlockSpec((None, r, a, m), lambda i: (i, 0, 0, 0))],
        out_specs=pl.BlockSpec((None, r * HALF, 2 * m), lambda i: (i, 0, 0)),
        cost_estimate=cost(83 * 10**9, 8 * filters.size),
        compiler_params=LIMIT,
    )(*operands, filters)


def input_grad_part(at_x, both, filter_spec, tables):
    a, _, count, r, m = both.shape
    names = ("first", "turn", "forward", "inverse", "last")
    specs, operands = table_specs(tables, names)
    spec_shape = (None, r * HALF, 2 * m)
    grid_spec = pltpu.PrefetchScalarGridSpec(
        num_scalar_prefetch=1,
        grid=(count,),
        in_specs=specs
        + [
            pl.BlockSpec((a, None, None, r, m), lambda i, at: (0, 0, i, 0, 0)),
            pl.BlockSpec(spec_shape, lambda i, at: ((at[0] - i) & (count - 1), 0, 0)),
        ],
        out_specs=[
            pl.BlockSpec(spec_shape, lambda i, at: (i, 0, 0)),
            pl.BlockSpec((a, None, r, m), lambda i, at: (0, i, 0, 0)),
        ],
    )
    return pl.pallas_call(
        input_grad_kernel,
        grid_spec=grid_spec,
        out_shape=[
            jax.ShapeDtypeStruct((count, r * HALF, 2 * m), jnp.float32),
            jax.ShapeDtypeStruct((a, count, r, m), jnp.float32),
        ],
        cost_estimate=cost(2 * 10**9, 8 * both.size),
        compiler_params=LIMIT,
    )(at_x, *operands, both, filter_spec)


def filter_grad_part(at_x, both, grad_spec, tables):
    a, _, count, r, m = both.shape
    names = ("first", "turn", "forward", "inverse", "last_scaled")
    specs, operands = table_specs(tables, names)
    grid_spec = pltpu.PrefetchScalarGridSpec(
        num_scalar_prefetch=1,
        grid=(count,),
        in_specs=specs
        + [
            pl.BlockSpec((a, None, None, r, m), lambda i, at: (0, 1, i, 0, 0)),
            pl.BlockSpec((None, r * HALF, 2 * m), lambda i, at: (i, 0, 0)),
        ],
        out_specs=pl.BlockSpec(
            (None, r, a, m), lambda i, at: ((i - at[0]) & (count - 1), 0, 0, 0)
        ),
    )
    return pl.pallas_call(
        filter_grad_kernel,
        grid_spec=grid_spec,
        out_shape=jax.ShapeDtypeStruct((count, r, a, m), jnp.float32),
        cost_estimate=cost(0, 0),
        compiler_params=LIMIT,
    )(at_x, *operands, both, grad_spec)


def in_parts(incoming, work, outgoing):
    for copies in incoming:
        for copy in copies:
            copy.start()
    for i, copies in enumerate(incoming):
        for copy in copies:
            copy.wait()
        work(i)
        outgoing[i].start()
    for copy in outgoing:
        copy.wait()


def pack_kernel(half, grad, tokens, blocks, arrived, leaving, in_sems, out_sems):
    _, _, y, z, rows, _ = tokens.shape
    own, far, j = half[0], 1 - half[0], rows // 2
    arrays = (grad, tokens)
    incoming = [
        [
            pltpu.make_async_copy(array.at[:, :, i], arrived.at[i, n], in_sems.at[i, n])
            for n, array in enumerate(arrays)
        ]
        for i in range(y)
    ]
    outgoing = [
        pltpu.make_async_copy(leaving.at[i], blocks.at[i], out_sems.at[i]) for i in range(y)
    ]

    def work(i):
        for k in range(z):
            for n in range(len(arrays)):
                near, other = arrived[i, n, :, own, k], arrived[i, n, :, far, z - 1 - k]
                leaving[i, k, 0, n] = jnp.concatenate([near[:, :j], other[:, :j]], axis=1)
                leaving[i, k, 1, n] = jnp.concatenate([near[:, j:], other[:, j:]], axis=1)

    in_parts(incoming, work, outgoing)


def unpack_kernel(half, blocks, tokens, arrived, leaving, in_sems, out_sems):
    y, z, _, _, rows, _ = blocks.shape
    own, far, j = half[0], 1 - half[0], rows // 2
    incoming = [
        [pltpu.make_async_copy(blocks.at[i], arrived.at[i], in_sems.at[i])] for i in range(y)
    ]
    outgoing = [
        pltpu.make_async_copy(leaving.at[i], tokens.at[:, :, i], out_sems.at[i])
        for i in range(y)
    ]

    def work(i):
        for k in range(z):
            low, high = arrived[i, k, 0], arrived[i, k, 1]
            leaving[i, :, own, k] = jnp.concatenate([low[:, :j], high[:, :j]], axis=1)
            leaving[i, :, far, z - 1 - k] = jnp.concatenate([low[:, j:], high[:, j:]], axis=1)

    in_parts(incoming, work, outgoing)


def moving(kernel, half, arrays, shape, scratch, sems):
    anywhere = pl.BlockSpec(memory_space=pl.ANY)
    return pl.pallas_call(
        kernel,
        out_shape=jax.ShapeDtypeStruct(shape, jnp.float32),
        in_specs=[pl.BlockSpec(memory_space=pltpu.SMEM)] + [anywhere] * len(arrays),
        out_specs=anywhere,
        scratch_shapes=[pltpu.VMEM(v, jnp.float32) for v in scratch]
        + [pltpu.SemaphoreType.DMA(v) for v in sems],
        cost_estimate=cost(0, 8 * math.prod(shape)),
    )(half, *arrays)


def pack(half, grad, tokens):
    x, h, y, z, rows, lanes = grad.shape
    shape = (y, z, 2, 2, x, rows, lanes)
    scratch = [(y, 2, x, h, z, rows, lanes), shape]
    return moving(pack_kernel, half, [grad, tokens], shape, scratch, [(y, 2), (y,)])


def unpack(half, blocks, shape):
    x, h, y, z, rows, lanes = shape
    scratch = [blocks.shape, (y, x, h, z, rows, lanes)]
    return moving(unpack_kernel, half, [blocks], shape, scratch, [(y,), (y,)])


def shards(inputs, grad_out, filters):
    x, h, y, z, c = (lax.axis_size(a) for a in ("x", "zh", "y", "zl", "c"))
    _, channels, block = inputs.shape
    j = channels // (x * h * y * z * c)
    seq_length = filters.shape[1]
    rows = y * z * c
    tables = dft_tables(seq_length, 1.0 / math.sqrt(x * h * seq_length))
    half = lax.axis_index("zh").reshape(1).astype(jnp.int32)
    at_x = lax.axis_index("x").reshape(1).astype(jnp.int32)
    whole_shape = (x, h, y, z, c * j, INNER)

    def exchange(blocks):
        return lax.all_to_all(blocks, ("y", "zl", "c"), 0, 0, tiled=True)

    def facing(v):
        return lax.ppermute(v, ("zh", "zl"), [(i, h * z - 1 - i) for i in range(h * z)])

    def along_x(v, s):
        return lax.ppermute(v, "x", [(i, (i + s) % x) for i in range(x)])

    both = pack(half, grad_out.reshape(whole_shape), inputs.reshape(whole_shape))
    both, filters = lax.optimization_barrier((both, filters))
    both = exchange(both.reshape(rows, 2, x, h * j, INNER))

    pair = jnp.concatenate([filters, facing(filters)]).reshape(h * j, rows, INNER)
    taps = jnp.stack([pair] + [along_x(pair, s) for s in range(1, x)])
    filter_spec = filter_spectrum(taps, tables)

    grad_spec, leaving = input_grad_part(at_x, both, filter_spec, tables)
    returned = exchange(leaving)

    parts = filter_grad_part(at_x, both, grad_spec, tables)
    part = parts[0] + sum(along_x(parts[s], s) for s in range(1, x))
    filter_grad = part[:j] + facing(part[j:])

    blocks = returned.reshape(y, z, c, x, h * j, INNER)
    input_grad = unpack(half, blocks, whole_shape)
    return (input_grad.reshape(1, channels, block), filter_grad.reshape(j, seq_length))


def solution(mesh):
    devices = mesh.devices.reshape(4, 2, 4, -1, 2)
    fine = Mesh(devices, ("x", "zh", "y", "zl", "c"))
    tokens = P(("x", "zh"), None, ("y", "zl", "c"))
    owners = P(("x", "zh", "y", "zl", "c"), None)
    return jax.shard_map(
        shards,
        mesh=fine,
        in_specs=(tokens, tokens, owners),
        out_specs=(tokens, owners),
        check_vma=False,
    )
```

```python
import math

import jax
import jax.numpy as jnp
import numpy as np
from jax import lax
from jax.experimental import pallas as pl
from jax.experimental.pallas import tpu as pltpu
from jax.sharding import Mesh
from jax.sharding import PartitionSpec as P

INNER = 128
HALF = 72


def three_parts(table, axis):
    high = np.asarray(table, np.float32).astype(jnp.bfloat16)
    low = (table - high.astype(np.float64)).astype(jnp.bfloat16)
    return jnp.asarray(np.concatenate([high, high, low], axis=axis))


def dft_tables(seq_length, norm):
    padded = 2 * seq_length
    outer = padded // INNER
    rows = seq_length // INNER
    freqs = outer // 2 + 1
    row, freq, inner = np.arange(rows), np.arange(freqs), np.arange(INNER)
    pad = ((0, HALF - freqs), (0, 0))
    angle = 2.0 * np.pi / outer * (freq[:, None] * row[None, :] % outer)
    cos_outer, sin_outer = np.pad(np.cos(angle), pad), np.pad(np.sin(angle), pad)
    weights = np.where((freq == 0) | (freq == freqs - 1), 1.0, 2.0)[:, None] / padded
    weights = np.pad(weights, pad)
    first = np.concatenate([cos_outer, -sin_outer], axis=0)
    last = np.concatenate([cos_outer * weights, -sin_outer * weights], axis=0).T
    angle = 2.0 * np.pi / INNER * (inner[:, None] * inner[None, :] % INNER)
    cos_inner, sin_inner = np.cos(angle), np.sin(angle)
    forward = np.block([[cos_inner, -sin_inner], [sin_inner, cos_inner]])
    inverse = np.block([[cos_inner, sin_inner], [-sin_inner, cos_inner]])
    angle = 2.0 * np.pi / padded * (freq[:, None] * inner[None, :] % padded)
    turn = np.stack([np.pad(np.cos(angle), pad), np.pad(np.sin(angle), pad)])
    left = dict(first=first, last=last, last_scaled=last * norm)
    right = dict(forward=forward, inverse=inverse)
    tables = {name: three_parts(t, 1) for name, t in left.items()}
    tables.update({name: three_parts(t, 0) for name, t in right.items()})
    tables["turn"] = jnp.asarray(turn, jnp.float32)
    return tables


def split(values):
    high = values.astype(jnp.bfloat16)
    return high, (values - high.astype(jnp.float32)).astype(jnp.bfloat16)


def dot(a, b):
    return jnp.dot(a, b, preferred_element_type=jnp.float32)


def forward_spectrum(wide, first, turn, forward):
    high, low = split(wide)
    outer = dot(first[...], jnp.concatenate([high, low, high], axis=0))
    cos, sin = turn[0], turn[1]
    turned = []
    for at in range(0, wide.shape[1], INNER):
        real, imag = outer[:HALF, at : at + INNER], outer[HALF:, at : at + INNER]
        turned.append(
            jnp.concatenate([real * cos + imag * sin, imag * cos - real * sin], axis=1)
        )
    high, low = split(jnp.concatenate(turned, axis=0))
    return dot(jnp.concatenate([high, low, high], axis=1), forward[...])


def correlate(spec, other):
    real, imag = spec[:, :INNER], spec[:, INNER:]
    other_real, other_imag = other[:, :INNER], other[:, INNER:]
    return jnp.concatenate(
        [real * other_real + imag * other_imag, imag * other_real - real * other_imag], axis=1
    )


def inverse_signal(spec, inverse, turn, last):
    high, low = split(spec)
    middle = dot(jnp.concatenate([high, low, high], axis=1), inverse[...])
    cos, sin = turn[0], turn[1]
    back = []
    for at in range(0, spec.shape[0], HALF):
        real, imag = middle[at : at + HALF, :INNER], middle[at : at + HALF, INNER:]
        back.append(
            jnp.concatenate([real * cos - imag * sin, imag * cos + real * sin], axis=0)
        )
    high, low = split(jnp.concatenate(back, axis=1))
    return dot(last[...], jnp.concatenate([high, low, high], axis=0))


def row(r, block):
    a, rows, _ = block.shape
    return pl.ds(r, a, stride=rows)


def rows_to_wide(block):
    a, rows, m = block.shape
    flat = block.reshape(a * rows, m)
    return jnp.concatenate([flat[row(r, block), :] for r in range(rows)], axis=1)


def pairs_to_wide(block):
    a, count, rows, m = block.shape
    flat, all_rows = block.reshape(a * count * rows, m), count * rows
    return jnp.concatenate(
        [flat[pl.ds(r, a, stride=all_rows), :] for r in range(all_rows)], axis=1
    )


def filter_kernel(first, turn, forward, filters, spec):
    wide = jnp.concatenate([filters[r] for r in range(filters.shape[0])], axis=1)
    spec[...] = forward_spectrum(wide, first, turn, forward)


def input_grad_kernel(at, first, turn, forward, inverse, last, grad, *refs):
    *filter_specs, spec, out = refs
    a, count, rows, m = out.shape
    wide = pairs_to_wide(grad)
    value = forward_spectrum(wide, first, turn, forward)
    size = rows * HALF
    for i in range(count):
        spec[i] = value[i * size : (i + 1) * size]
    other = jnp.concatenate([v[...] for v in filter_specs], axis=0)
    wide = inverse_signal(correlate(value, other), inverse, turn, last)
    flat = out.reshape(a * count * rows, m)
    for i in range(count):
        for r in range(rows):
            at_row = (i * rows + r) * INNER
            flat[pl.ds(i * rows + r, a, stride=count * rows), :] = wide[:, at_row : at_row + INNER]


def filter_grad_kernel(at, first, turn, forward, inverse, last, tokens, grad_spec, out):
    spec = forward_spectrum(rows_to_wide(tokens), first, turn, forward)
    wide = inverse_signal(correlate(grad_spec[...], spec), inverse, turn, last)
    for r in range(out.shape[0]):
        out[r] = wide[:, r * INNER : (r + 1) * INNER]


def table_specs(tables, names):
    whole = lambda t: pl.BlockSpec(t.shape, lambda i, *_: (0,) * t.ndim)
    return [whole(tables[n]) for n in names], [tables[n] for n in names]


def cost(flops, size):
    return pl.CostEstimate(flops=flops, bytes_accessed=size, transcendentals=0)


LIMIT = pltpu.CompilerParams(vmem_limit_bytes=48 * 2**20)


def filter_spectrum(filters, tables):
    count, r, a, m = filters.shape
    specs, operands = table_specs(tables, ("first", "turn", "forward"))
    return pl.pallas_call(
        filter_kernel,
        grid=(count,),
        out_shape=jax.ShapeDtypeStruct((count, r * HALF, 2 * m), jnp.float32),
        in_specs=specs + [pl.BlockSpec((None, r, a, m), lambda i: (i, 0, 0, 0))],
        out_specs=pl.BlockSpec((None, r * HALF, 2 * m), lambda i: (i, 0, 0)),
        cost_estimate=cost(83 * 10**9, 8 * filters.size),
        compiler_params=LIMIT,
    )(*operands, filters)


def input_grad_part(at_x, both, filter_spec, tables):
    a, _, count, r, m = both.shape
    names = ("first", "turn", "forward", "inverse", "last")
    specs, operands = table_specs(tables, names)
    spec_shape = (None, r * HALF, 2 * m)
    grid_spec = pltpu.PrefetchScalarGridSpec(
        num_scalar_prefetch=1,
        grid=(count // 2,),
        in_specs=specs
        + [
            pl.BlockSpec((a, None, 2, r, m), lambda i, at: (0, 0, i, 0, 0)),
            pl.BlockSpec(spec_shape, lambda i, at: ((at[0] - 2 * i) & (count - 1), 0, 0)),
            pl.BlockSpec(spec_shape, lambda i, at: ((at[0] - 2 * i - 1) & (count - 1), 0, 0)),
        ],
        out_specs=[
            pl.BlockSpec((2, r * HALF, 2 * m), lambda i, at: (i, 0, 0)),
            pl.BlockSpec((a, 2, r, m), lambda i, at: (0, i, 0, 0)),
        ],
    )
    return pl.pallas_call(
        input_grad_kernel,
        grid_spec=grid_spec,
        out_shape=[
            jax.ShapeDtypeStruct((count, r * HALF, 2 * m), jnp.float32),
            jax.ShapeDtypeStruct((a, count, r, m), jnp.float32),
        ],
        cost_estimate=cost(2 * 10**9, 8 * both.size),
        compiler_params=LIMIT,
    )(at_x, *operands, both, filter_spec, filter_spec)


def filter_grad_part(at_x, both, grad_spec, tables):
    a, _, count, r, m = both.shape
    names = ("first", "turn", "forward", "inverse", "last_scaled")
    specs, operands = table_specs(tables, names)
    grid_spec = pltpu.PrefetchScalarGridSpec(
        num_scalar_prefetch=1,
        grid=(count,),
        in_specs=specs
        + [
            pl.BlockSpec((a, None, None, r, m), lambda i, at: (0, 1, i, 0, 0)),
            pl.BlockSpec((None, r * HALF, 2 * m), lambda i, at: (i, 0, 0)),
        ],
        out_specs=pl.BlockSpec(
            (None, r, a, m), lambda i, at: ((i - at[0]) & (count - 1), 0, 0, 0)
        ),
    )
    return pl.pallas_call(
        filter_grad_kernel,
        grid_spec=grid_spec,
        out_shape=jax.ShapeDtypeStruct((count, r, a, m), jnp.float32),
        cost_estimate=cost(0, 0),
        compiler_params=LIMIT,
    )(at_x, *operands, both, grad_spec)


def in_parts(incoming, work, outgoing):
    for copies in incoming:
        for copy in copies:
            copy.start()
    for i, copies in enumerate(incoming):
        for copy in copies:
            copy.wait()
        work(i)
        outgoing[i].start()
    for copy in outgoing:
        copy.wait()


def pack_kernel(half, grad, tokens, blocks, arrived, leaving, in_sems, out_sems):
    _, _, y, z, rows, _ = tokens.shape
    own, far, j = half[0], 1 - half[0], rows // 2
    arrays = (grad, tokens)
    incoming = [
        [
            pltpu.make_async_copy(array.at[:, :, i], arrived.at[i, n], in_sems.at[i, n])
            for n, array in enumerate(arrays)
        ]
        for i in range(y)
    ]
    outgoing = [
        pltpu.make_async_copy(leaving.at[i], blocks.at[i], out_sems.at[i]) for i in range(y)
    ]

    def work(i):
        for k in range(z):
            for n in range(len(arrays)):
                near, other = arrived[i, n, :, own, k], arrived[i, n, :, far, z - 1 - k]
                leaving[i, k, 0, n] = jnp.concatenate([near[:, :j], other[:, :j]], axis=1)
                leaving[i, k, 1, n] = jnp.concatenate([near[:, j:], other[:, j:]], axis=1)

    in_parts(incoming, work, outgoing)


def unpack_kernel(half, blocks, tokens, arrived, leaving, in_sems, out_sems):
    y, z, _, _, rows, _ = blocks.shape
    own, far, j = half[0], 1 - half[0], rows // 2
    incoming = [
        [pltpu.make_async_copy(blocks.at[i], arrived.at[i], in_sems.at[i])] for i in range(y)
    ]
    outgoing = [
        pltpu.make_async_copy(leaving.at[i], tokens.at[:, :, i], out_sems.at[i])
        for i in range(y)
    ]

    def work(i):
        for k in range(z):
            low, high = arrived[i, k, 0], arrived[i, k, 1]
            leaving[i, :, own, k] = jnp.concatenate([low[:, :j], high[:, :j]], axis=1)
            leaving[i, :, far, z - 1 - k] = jnp.concatenate([low[:, j:], high[:, j:]], axis=1)

    in_parts(incoming, work, outgoing)


def moving(kernel, half, arrays, shape, scratch, sems):
    anywhere = pl.BlockSpec(memory_space=pl.ANY)
    return pl.pallas_call(
        kernel,
        out_shape=jax.ShapeDtypeStruct(shape, jnp.float32),
        in_specs=[pl.BlockSpec(memory_space=pltpu.SMEM)] + [anywhere] * len(arrays),
        out_specs=anywhere,
        scratch_shapes=[pltpu.VMEM(v, jnp.float32) for v in scratch]
        + [pltpu.SemaphoreType.DMA(v) for v in sems],
        cost_estimate=cost(0, 8 * math.prod(shape)),
    )(half, *arrays)


def pack(half, grad, tokens):
    x, h, y, z, rows, lanes = grad.shape
    shape = (y, z, 2, 2, x, rows, lanes)
    scratch = [(y, 2, x, h, z, rows, lanes), shape]
    return moving(pack_kernel, half, [grad, tokens], shape, scratch, [(y, 2), (y,)])


def unpack(half, blocks, shape):
    x, h, y, z, rows, lanes = shape
    scratch = [blocks.shape, (y, x, h, z, rows, lanes)]
    return moving(unpack_kernel, half, [blocks], shape, scratch, [(y,), (y,)])


def shards(inputs, grad_out, filters):
    x, h, y, z, c = (lax.axis_size(a) for a in ("x", "zh", "y", "zl", "c"))
    _, channels, block = inputs.shape
    j = channels // (x * h * y * z * c)
    seq_length = filters.shape[1]
    rows = y * z * c
    tables = dft_tables(seq_length, 1.0 / math.sqrt(x * h * seq_length))
    half = lax.axis_index("zh").reshape(1).astype(jnp.int32)
    at_x = lax.axis_index("x").reshape(1).astype(jnp.int32)
    whole_shape = (x, h, y, z, c * j, INNER)

    def exchange(blocks):
        return lax.all_to_all(blocks, ("y", "zl", "c"), 0, 0, tiled=True)

    def facing(v):
        return lax.ppermute(v, ("zh", "zl"), [(i, h * z - 1 - i) for i in range(h * z)])

    def along_x(v, s):
        return lax.ppermute(v, "x", [(i, (i + s) % x) for i in range(x)])

    both = pack(half, grad_out.reshape(whole_shape), inputs.reshape(whole_shape))
    both, filters = lax.optimization_barrier((both, filters))
    both = exchange(both.reshape(rows, 2, x, h * j, INNER))

    pair = jnp.concatenate([filters, facing(filters)]).reshape(h * j, rows, INNER)
    taps = jnp.stack([pair] + [along_x(pair, s) for s in range(1, x)])
    filter_spec = filter_spectrum(taps, tables)

    grad_spec, leaving = input_grad_part(at_x, both, filter_spec, tables)
    returned = exchange(leaving)

    parts = filter_grad_part(at_x, both, grad_spec, tables)
    part = parts[0] + sum(along_x(parts[s], s) for s in range(1, x))
    filter_grad = part[:j] + facing(part[j:])

    blocks = returned.reshape(y, z, c, x, h * j, INNER)
    input_grad = unpack(half, blocks, whole_shape)
    return (input_grad.reshape(1, channels, block), filter_grad.reshape(j, seq_length))


def solution(mesh):
    devices = mesh.devices.reshape(4, 2, 4, -1, 2)
    fine = Mesh(devices, ("x", "zh", "y", "zl", "c"))
    tokens = P(("x", "zh"), None, ("y", "zl", "c"))
    owners = P(("x", "zh", "y", "zl", "c"), None)
    return jax.shard_map(
        shards,
        mesh=fine,
        in_specs=(tokens, tokens, owners),
        out_specs=(tokens, owners),
        check_vma=False,
    )
```
